512 devices in a mesh: facet: 64 (over x_hi, z, core), col: 8 (over x_lo, y).
Axes of the slice: x: 4 (x_hi: 2, x_lo: 2; x = x_hi * 2 + x_lo), y: 4, z: 16, core: 2. Of those that a mesh axis runs over, the one named last changes fastest.
Arguments:
- facet_strips: bfloat16 [64, 2, 8192, 128], P('facet', None, 'col'), may hold values from -6 to 6
- facet_offsets: int32 [64, 2], P('facet'), may hold values from 0 to 65535
- column_offsets: int32 [8], P('col'), may hold values from 0 to 65535
- row_offsets: int32 [1], replicated, may hold values from 0 to 65535
- tile_lists: int32 [8, 64, 8], P('col', 'facet'), may hold values from 0 to 63
- tile_counts: int32 [8, 64], P('col', 'facet'), may hold values from 1 to 8, 256 in all within a row
- uv_index: int32 [8, 64, 8, 2, 1024], P('col', 'facet'), may hold values from 0 to 4095
Outputs:
- visibilities: float32 [8, 64, 8, 2, 1024], P('col', 'facet')
The draws below stay inside these ranges and needn't reach their ends.
Inputs may be any that keep to these rules, and one draw needn't show every extreme that they name: `tile_counts`: each column has an owner whose count is exactly 8.
All inputs are finite; a program needn't handle non-finite values. No bound on the sum of `tile_counts` on one device may be relied on, other than what follows from the above.
Results may differ from the reference program's by a relative error of at most 0.0058.
Values may be sent and summed in bfloat16 or wider, within the bound.
A program may use at most 64 MiB of HBM per device.

```python
import math
import jax
import jax.numpy as jnp
import numpy as np
from jax import lax

L = 8192
W = 128
S = 256
TILE = 32
NTOT = 65536
UV_STEPS = 4096
VIS = 1024
CAP = 8
ROWS = 1
FACETS = 64
COLS = 8
OWNERS = 64
TILE_IDS = 64


def touch_ends(array, key, least, largest):
    place = [jax.random.randint(jax.random.fold_in(key, axis), (), 0, length) for axis, length in enumerate(array.shape)]
    widest = array.shape.index(max(array.shape))
    next_to = place[:widest] + [(place[widest] + 1) % array.shape[widest]] + place[widest + 1:]
    return array.at[tuple(place)].set(least).at[tuple(next_to)].set(largest)


def block_levels(stream_key, dims, pieces, smallest, high):
    def one(dim, blocks):
        draws = jax.random.uniform(jax.random.fold_in(jax.random.fold_in(stream_key, 6), dim), (blocks,), jnp.float32, smallest / len(pieces), high / len(pieces))
        return jnp.repeat(jnp.exp(draws), dims[dim] // blocks).reshape((-1,) + (1,) * (len(dims) - dim - 1))

    gain = one(*pieces[0])
    for cut in pieces[1:]:
        gain = gain * one(*cut)
    return gain


def length_profile(count, total, bound, lean):
    weights = [(1 << 20) // math.isqrt(standing ** lean) + 1 for standing in range(2, count + 1)]
    spare, counts = total - bound - (count - 1), [1] * (count - 1)
    while spare > 0:
        movable = [i for i in range(count - 1) if counts[i] < bound]
        pool, remaining = sum([weights[i] for i in movable]), spare
        for i in movable:
            addition = min(bound - counts[i], max(1, remaining * weights[i] // pool), spare)
            counts[i] = counts[i] + addition
            spare = spare - addition
    return np.array([bound] + counts)


def ragged(own_key, number_of, total, bound, lean):
    if number_of == 2:
        one = jax.random.randint(own_key, (), max(1, total - bound), min(bound, total - 1) + 1)
        return jnp.stack([one, total - one])
    tallies = jnp.asarray(length_profile(number_of, total, bound, lean), jnp.int32)
    twos = (number_of - 1) // 2
    source_of, taker = tallies[1:1 + 2 * twos:2], tallies[2:2 + 2 * twos:2]
    room = jnp.minimum(source_of - 1, bound - taker)
    moved = jax.random.randint(jax.random.fold_in(own_key, 1), (twos,), 0, 1 << 20) % (room + 1)
    tallies = tallies.at[1:1 + 2 * twos:2].set(source_of - moved).at[2:2 + 2 * twos:2].set(taker + moved)
    return tallies[jax.random.permutation(jax.random.fold_in(own_key, 2), number_of)]


def centred(rng, dims, width, bound, pieces=(), kind=jnp.bfloat16):
    result = jax.random.normal(rng, dims, jnp.float32) * width
    if len(pieces) > 0:
        result = block_levels(rng, dims, pieces, -0.22, 0.18) * result
    return jnp.clip(result, min=-bound, max=bound).astype(kind)


def setup_inputs(seed: int = 0) -> dict:
    keys = jax.random.split(jax.random.key(seed), 8)
    facet_strips = centred(keys[0], (FACETS, 2, L, W), 1.0, 6.0, ((0, 64), (2, 8)))
    facet_offsets = touch_ends(jax.random.randint(keys[1], (FACETS, 2), 0, NTOT), jax.random.fold_in(keys[1], 1), 0, NTOT - 1).astype(jnp.int32)
    column_offsets = touch_ends(jax.random.randint(keys[2], (COLS,), 0, NTOT), jax.random.fold_in(keys[2], 1), 0, NTOT - 1).astype(jnp.int32)
    row_offsets = jax.random.randint(keys[3], (ROWS,), 0, NTOT).astype(jnp.int32)
    tile_lists = touch_ends(jax.random.randint(keys[4], (COLS, OWNERS, CAP), 0, TILE_IDS), jax.random.fold_in(keys[4], 1), 0, TILE_IDS - 1).astype(jnp.int32)
    tile_counts = jax.vmap(lambda own: ragged(own, OWNERS, OWNERS * CAP // 2, CAP, 2))(jax.random.split(keys[5], COLS)).reshape((COLS, OWNERS)).astype(jnp.int32)
    uv_index = touch_ends(jax.random.randint(keys[6], (COLS, OWNERS, CAP, 2, VIS), 0, UV_STEPS), jax.random.fold_in(keys[6], 1), 0, UV_STEPS - 1).astype(jnp.int32)
    return {"facet_strips": facet_strips, "facet_offsets": facet_offsets, "column_offsets": column_offsets, "row_offsets": row_offsets, "tile_lists": tile_lists, "tile_counts": tile_counts, "uv_index": uv_index}


def mod_product(first, second):
    high = first // 256
    low = first % 256
    return (high * (second * 256 % NTOT) + low * second) % NTOT

def phase_parts(row_start, row_count, row_step, col_start, col_count, col_step):
    left_side = ((row_start + row_step * jnp.arange(row_count, dtype=jnp.int32)) % NTOT)[:, None]
    right_side = ((col_start + col_step * jnp.arange(col_count, dtype=jnp.int32)) % NTOT)[None, :]
    index = mod_product(left_side, right_side)
    angle = index.astype(jnp.float32) * (2.0 * math.pi / NTOT)
    return (jnp.cos(angle), jnp.sin(angle))

def left_operator(row_start, col_start, count):
    cosine, sine = phase_parts(row_start, S, NTOT // L, col_start, count, 1)
    upper = jnp.concatenate([cosine, sine], axis=1)
    lower = jnp.concatenate([-sine, cosine], axis=1)
    return (jnp.concatenate([upper, lower], axis=0) * (1.0 / math.sqrt(L))).astype(jnp.bfloat16)

def right_operator(column_start, strip_start):
    cosine, sine = phase_parts(strip_start, W, 1, column_start, S, NTOT // S)
    table = jnp.stack([jnp.stack([cosine, -sine], axis=1), jnp.stack([sine, cosine], axis=1)])
    table = table * (1.0 / math.sqrt(W))
    return table.reshape(2, W, 2, S // TILE, TILE).astype(jnp.bfloat16)

def tile_terms(strip_rows, table):
    count = strip_rows.shape[0]
    shaped = strip_rows.reshape(count, 2, S // TILE, TILE, W).astype(jnp.float32)
    terms = jnp.einsum('rkapw,kwjbq->abrjpq', shaped, table.astype(jnp.float32), preferred_element_type=jnp.float32)
    return terms.reshape((S // TILE) ** 2, count, 2, TILE * TILE)

def select_tiles(flat_tiles, identity, live):
    slots = jnp.arange(identity.shape[0], dtype=jnp.int32)
    ids = jnp.arange(flat_tiles.shape[0], dtype=jnp.int32)
    onehot = ((identity[:, None] == ids[None, :]) & (slots[:, None] < live)).astype(jnp.bfloat16)
    return jnp.dot(onehot, flat_tiles, preferred_element_type=jnp.float32).astype(jnp.bfloat16)

def visibilities_of(chosen, uv_slots):
    slots = chosen.shape[0]
    tiles = chosen.astype(jnp.float32).reshape(slots, 2, TILE, TILE)
    pixels = jnp.arange(TILE, dtype=jnp.int32)
    factor = 2.0 * math.pi / UV_STEPS
    u_angle = (uv_slots[:, 0, None, :] * pixels[None, :, None] % UV_STEPS).astype(jnp.float32) * factor
    v_angle = (uv_slots[:, 1, None, :] * pixels[None, :, None] % UV_STEPS).astype(jnp.float32) * factor
    u_cos, u_sin = (jnp.cos(u_angle), jnp.sin(u_angle))
    v_cos, v_sin = (jnp.cos(v_angle), jnp.sin(v_angle))
    high = lax.Precision.HIGHEST
    real_mid = jnp.einsum('cpq,cqk->cpk', tiles[:, 0], v_cos, precision=high) - jnp.einsum('cpq,cqk->cpk', tiles[:, 1], v_sin, precision=high)
    imag_mid = jnp.einsum('cpq,cqk->cpk', tiles[:, 0], v_sin, precision=high) + jnp.einsum('cpq,cqk->cpk', tiles[:, 1], v_cos, precision=high)
    real_vis = lax.optimization_barrier(jnp.sum(u_cos * real_mid - u_sin * imag_mid, axis=1)) / TILE
    imag_vis = lax.optimization_barrier(jnp.sum(u_cos * imag_mid + u_sin * real_mid, axis=1)) / TILE
    return jnp.stack([real_vis, imag_vis], axis=1)

def reference(facet_strips, facet_offsets, column_offsets, row_offsets, tile_lists, tile_counts, uv_index):

    def facet_rows(index):
        flat = facet_strips[index].reshape(2 * L, W)
        parts = [jnp.dot(left_operator(row_offsets[r], facet_offsets[index, 0], L), flat, preferred_element_type=jnp.float32).astype(jnp.bfloat16) for r in range(ROWS)]
        return jnp.stack(parts)
    rows_all = lax.map(facet_rows, jnp.arange(FACETS, dtype=jnp.int32))
    scale = 1.0 / math.sqrt(FACETS)
    outputs = []
    for column in range(COLS):

        def add_facet(carry, index):
            table = right_operator(column_offsets[column], facet_offsets[index, 1])
            return (carry + tile_terms(rows_all[index], table) * scale, None)
        start = jnp.zeros(((S // TILE) ** 2, ROWS, 2, TILE * TILE), jnp.float32)
        total, unused = lax.scan(add_facet, start, jnp.arange(FACETS, dtype=jnp.int32))
        flat_tiles = total.astype(jnp.bfloat16).reshape((S // TILE) ** 2 * ROWS, 2 * TILE * TILE)

        def owner_vis(owner):
            chosen = select_tiles(flat_tiles, tile_lists[column, owner], tile_counts[column, owner])
            return visibilities_of(chosen.reshape(-1, 2, TILE * TILE), uv_index[column, owner])
        outputs.append(lax.map(owner_vis, jnp.arange(OWNERS, dtype=jnp.int32)))
    return jnp.stack(outputs)
```

```python
import math

import jax
import jax.numpy as jnp
from jax import lax
from jax.experimental import pallas as pl
from jax.experimental.pallas import tpu as pltpu
from jax.sharding import PartitionSpec as P

L = 8192
W = 128
S = 256
TILE = 32
NTOT = 65536
UV_STEPS = 4096
VIS = 1024
CAP = 8
FACETS = 64
LEN = 1024
MESH = pl.DeviceIdType.MESH
F32 = jnp.float32
BF16 = jnp.bfloat16
I32 = jnp.int32


def unit(index):
    index = index & (NTOT - 1)
    index = jnp.where(index >= NTOT // 2, index - NTOT, index)
    angle = index.astype(F32) * (2.0 * math.pi / NTOT)
    return jnp.cos(angle), jnp.sin(angle)


def cmul(a, b):
    return a[0] * b[0] - a[1] * b[1], a[0] * b[1] + a[1] * b[0]


def iota(shape, dim):
    return lax.broadcasted_iota(I32, shape, dim)


def facet_of(x_hi, z, core):
    return (x_hi * 16 + z) * 2 + core


def group_facet(g, zg):
    return facet_of(g // 4, 2 * zg + g % 2, (g // 2) % 2)


def kernel(
    strip_ref,
    offsets_ref,
    column_ref,
    row_ref,
    lists_ref,
    counts_ref,
    uv_ref,
    out_ref,
    strip_v,
    uv_v,
    left_v,
    send1,
    recv1,
    block2,
    recv2,
    table_v,
    send3,
    recv3,
    recv4,
    small_v,
    recv_s,
    pick_v,
    send5,
    recv5,
    pow_v,
    u_v,
    v_v,
    load_sem,
    s_s,
    r_s,
    s_1,
    r_1,
    s_2,
    r_2,
    s_3,
    r_3,
    s_4,
    r_4,
    s_5,
    r_5,
):
    facet = lax.axis_index("facet")
    col = lax.axis_index("col")
    x_hi = facet // 32
    z = (facet // 2) % 16
    core = facet % 2
    zg = z // 2
    zp = z % 2
    q_me = x_hi * 2 + core
    g_me = q_me * 2 + zp
    place = 8 * zp + zg

    loads = [
        pltpu.make_async_copy(strip_ref.at[0, 0], strip_v.at[:, pl.ds(0, W)], load_sem.at[0]),
        pltpu.make_async_copy(strip_ref.at[0, 1], strip_v.at[:, pl.ds(W, W)], load_sem.at[1]),
        pltpu.make_async_copy(uv_ref.at[0, 0], uv_v, load_sem.at[2]),
    ]
    for load in loads:
        load.start()

    barrier = pltpu.get_barrier_semaphore()

    def greet(f, c):
        pl.semaphore_signal(barrier, inc=1, device_id=(f, c), device_id_type=MESH)

    @pl.loop(1, 8)
    def _(i):
        greet(facet, (col + i) % 8)

    @pl.loop(1, 8)
    def _(i):
        greet(group_facet((g_me + i) % 8, zg), col)

    @pl.loop(1, 16)
    def _(i):
        @pl.when((z + i) % 16 != 2 * zg + (1 - zp))
        def _():
            greet(facet_of(x_hi, (z + i) % 16, core), col)

    @pl.when(col != g_me)
    def _():
        @pl.loop(0, 8)
        def _(g):
            greet(group_facet(g, zg), g_me)

    row0 = row_ref[0]
    cells = offsets_ref[0, 0] + col * LEN + iota((8, LEN), 1)
    base = unit((row0 + 8 * iota((8, LEN), 0)) * cells)
    scale = 1.0 / math.sqrt(L)
    step = unit(64 * cells)

    def left_body(t, value):
        nxt = cmul(value, step)
        at = pl.ds(pl.multiple_of(16 * t, 16), 16)
        left_v[at, :] = jnp.concatenate([value[0], nxt[0]], axis=0).astype(BF16)
        at = pl.ds(pl.multiple_of(S + 16 * t, 16), 16)
        left_v[at, :] = jnp.concatenate([value[1], nxt[1]], axis=0).astype(BF16)
        return cmul(nxt, step)

    lax.fori_loop(0, 16, left_body, (base[0] * scale, base[1] * scale))

    loads[0].wait()
    loads[1].wait()
    both = jnp.dot(left_v[...], strip_v[...], preferred_element_type=F32)
    real = both[:S, :W] + both[S:, W:]
    imag = both[:S, W:] - both[S:, :W]
    send1[...] = jnp.concatenate([real, imag], axis=1).astype(BF16).reshape(8, 32, 2 * W)

    pl.semaphore_wait(barrier, 35)

    def copy1(c):
        return pltpu.make_async_remote_copy(
            src_ref=send1.at[c], dst_ref=recv1.at[col], send_sem=s_1.at[c], recv_sem=r_1.at[col],
            device_id=(facet, c), device_id_type=MESH,
        )

    def from1(c):
        return pltpu.make_async_remote_copy(
            src_ref=send1.at[c], dst_ref=recv1.at[c], send_sem=s_1.at[c], recv_sem=r_1.at[c],
            device_id=(facet, c), device_id_type=MESH,
        )

    @pl.loop(1, 8)
    def _(i):
        copy1((col + i) % 8).start()

    recv1[pl.ds(col, 1)] = send1[pl.ds(col, 1)]

    lanes = iota((8, W), 0)
    ids = jnp.full((8, W), -1, I32)
    for j in range(CAP):
        ids = jnp.where((lanes == j) & (j < counts_ref[0, 0]), lists_ref[0, 0, j], ids)
    small_v[0:8, :] = ids
    small_v[8:16, :] = jnp.full((8, W), offsets_ref[0, 1], I32)
    recv_s[pl.ds(g_me, 1)] = small_v[...][None]

    def copy_s(g, dst):
        return pltpu.make_async_remote_copy(
            src_ref=small_v, dst_ref=recv_s.at[dst], send_sem=s_s.at[g], recv_sem=r_s.at[dst],
            device_id=(group_facet(g, zg), col), device_id_type=MESH,
        )

    @pl.loop(1, 8)
    def _(i):
        copy_s((g_me + i) % 8, g_me).start()

    lane = iota((8, 2 * S), 1)
    sample = column_ref[0] + 256 * (32 * (lane // 64) + lane % 32)
    quarter = (NTOT // 4) * ((lane // 32) % 2)
    base_r = unit(iota((8, 2 * S), 0) * sample + quarter)
    step_r = unit(8 * sample)

    def right_body(t, value):
        nxt = cmul(value, step_r)
        re = jnp.concatenate([value[0], nxt[0]], axis=0)
        im = jnp.concatenate([value[1], nxt[1]], axis=0)
        top = pl.ds(pl.multiple_of(16 * t, 16), 16)
        low = pl.ds(pl.multiple_of(W + 16 * t, 16), 16)
        table_v[top, 0 : 2 * S] = re.astype(BF16)
        table_v[low, 0 : 2 * S] = im.astype(BF16)
        table_v[top, 2 * S :] = (-im).astype(BF16)
        table_v[low, 2 * S :] = re.astype(BF16)
        return cmul(nxt, step_r)

    lax.fori_loop(0, 8, right_body, base_r)

    @pl.loop(1, 8)
    def _(i):
        from1((col + i) % 8).wait_recv()

    total = recv1[0].astype(F32)
    for c in range(1, 8):
        total = total + recv1[c].astype(F32)
    block2[...] = total.astype(BF16)

    def copy2(c):
        return pltpu.make_async_remote_copy(
            src_ref=block2, dst_ref=recv2.at[g_me], send_sem=s_2.at[c], recv_sem=r_2.at[g_me],
            device_id=(group_facet(col, zg), c), device_id_type=MESH,
        )

    def from2(g):
        return pltpu.make_async_remote_copy(
            src_ref=block2, dst_ref=recv2.at[g], send_sem=s_2.at[g], recv_sem=r_2.at[g],
            device_id=(group_facet(g, zg), g_me), device_id_type=MESH,
        )

    @pl.when(col == g_me)
    def _():
        recv2[pl.ds(g_me, 1)] = block2[...][None]

    @pl.when(col != g_me)
    def _():
        copy2(col).start()

    @pl.loop(1, 8)
    def _(i):
        copy2((col + i) % 8).start()

    loads[2].wait()
    for part in range(2):
        index = jnp.concatenate([uv_v[j, part : part + 1, :] for j in range(CAP)], axis=0)
        value = unit(index * (NTOT // UV_STEPS))
        for k in range(5):
            pow_v[part, k, 0] = value[0]
            pow_v[part, k, 1] = value[1]
            value = cmul(value, value)

    sub = iota((8, VIS), 0)

    def powers(part, j):
        def power(k):
            return tuple(
                jnp.broadcast_to(pow_v[part, k, h, pl.ds(j, 1), :], (8, VIS)) for h in range(2)
            )

        def chosen_power(k):
            re, im = power(k)
            on = (sub & (1 << k)) != 0
            return jnp.where(on, re, 1.0), jnp.where(on, im, 0.0)

        low = cmul(cmul(chosen_power(0), chosen_power(1)), chosen_power(2))
        sixteen = power(4)
        second = cmul(low, power(3))
        third = cmul(low, sixteen)
        fourth = cmul(second, sixteen)
        parts = (low, second, third, fourth)
        return tuple(jnp.concatenate([p[h] for p in parts], axis=0) for h in range(2))

    @pl.loop(0, CAP)
    def _(j):
        re, im = powers(0, j)
        u_v[0, j] = re * (1.0 / TILE)
        u_v[1, j] = im * (1.0 / TILE)
        re, im = powers(1, j)
        top = pl.ds(pl.multiple_of(64 * j, 32), 32)
        low = pl.ds(pl.multiple_of(64 * j + 32, 32), 32)
        v_v[top, 0:VIS] = re.astype(BF16)
        v_v[top, VIS:] = im.astype(BF16)
        v_v[low, 0:VIS] = (-im).astype(BF16)
        v_v[low, VIS:] = re.astype(BF16)

    @pl.loop(1, 8)
    def _(i):
        copy_s((g_me + i) % 8, (g_me + i) % 8).wait_recv()

    across = jnp.zeros((8, W), I32)
    for g in range(8):
        across = jnp.where(lanes == g, recv_s[g, 8:16, :], across)
    across = jnp.concatenate([across] * 4, axis=1)
    turn = unit(across * sample)
    norm = 1.0 / math.sqrt(W * FACETS)
    turn = (turn[0] * norm, turn[1] * norm)

    entry = iota((16, 2 * W), 1)
    diagonal = iota((16, 2 * W), 0) == entry % 16
    entry = 16 * q_me + entry // 16

    @pl.loop(0, 4)
    def _(q):
        for j in range(CAP):
            wanted = recv_s[2 * q + zp, j : j + 1, :]
            wanted = jnp.broadcast_to(jnp.concatenate([wanted, wanted], axis=1), (16, 2 * W))
            pick = jnp.where((wanted == entry) & diagonal, 1.0, 0.0)
            pick_v[q, 16 * j : 16 * j + 16, :] = pick.astype(BF16)

    @pl.when(col == g_me)
    def _():
        @pl.loop(1, 8)
        def _(i):
            from2((g_me + i) % 8).wait_recv()

    @pl.when(col != g_me)
    def _():
        @pl.loop(0, 8)
        def _(g):
            from2(g).wait_recv()

    grid = jnp.dot(
        recv2[...].reshape(8 * 32, 2 * W), table_v[...], preferred_element_type=F32
    )
    terms = None
    for g in range(8):
        rows = grid[32 * g : 32 * g + 32]
        term = rows[:, : 2 * S] * turn[0][g : g + 1] + rows[:, 2 * S :] * turn[1][g : g + 1]
        terms = term if terms is None else terms + term

    low_half = iota((16, W), 1) < 64
    for v in range(4):
        top = terms[0:16, W * v : W * v + W]
        low = terms[16:32, W * v : W * v + W]
        send3[2 * v] = jnp.where(low_half, top, pltpu.roll(low, 64, 1)).astype(BF16)
        send3[2 * v + 1] = jnp.where(low_half, pltpu.roll(top, 64, 1), low).astype(BF16)

    def copy3(b, dst):
        return pltpu.make_async_remote_copy(
            src_ref=send3.at[b], dst_ref=recv3.at[dst], send_sem=s_3.at[b], recv_sem=r_3.at[dst],
            device_id=(facet_of(x_hi, 2 * b + zp, core), col), device_id_type=MESH,
        )

    @pl.loop(1, 8)
    def _(i):
        copy3((zg + i) % 8, zg).start()

    recv3[pl.ds(zg, 1)] = send3[pl.ds(zg, 1)]

    @pl.loop(1, 8)
    def _(i):
        copy3((zg + i) % 8, (zg + i) % 8).wait_recv()

    total = recv3[0].astype(F32)
    for b in range(1, 8):
        total = total + recv3[b].astype(F32)
    recv4[pl.ds(place, 1)] = total.astype(BF16)[None]

    def copy4(n, dst):
        return pltpu.make_async_remote_copy(
            src_ref=recv4.at[place], dst_ref=recv4.at[dst], send_sem=s_4.at[n], recv_sem=r_4.at[dst],
            device_id=(facet_of(x_hi, 2 * (n % 8) + n // 8, core), col), device_id_type=MESH,
        )

    @pl.loop(1, 16)
    def _(i):
        copy4((place + i) % 16, place).start()

    @pl.loop(1, 16)
    def _(i):
        copy4((place + i) % 16, (place + i) % 16).wait_recv()

    picks = jnp.dot(
        pick_v[...].reshape(4 * W, 2 * W), recv4[...].reshape(2 * W, W), preferred_element_type=F32
    )
    send5[...] = picks.astype(BF16).reshape(4, W, W)

    def copy5(q, dst):
        return pltpu.make_async_remote_copy(
            src_ref=send5.at[q], dst_ref=recv5.at[dst], send_sem=s_5.at[q], recv_sem=r_5.at[dst],
            device_id=(facet_of(q // 2, z, q % 2), col), device_id_type=MESH,
        )

    @pl.loop(1, 4)
    def _(i):
        copy5((q_me + i) % 4, q_me).start()

    recv5[pl.ds(q_me, 1)] = send5[pl.ds(q_me, 1)]

    @pl.loop(1, 4)
    def _(i):
        copy5((q_me + i) % 4, (q_me + i) % 4).wait_recv()

    chosen = recv5[0].astype(F32)
    for q in range(1, 4):
        chosen = chosen + recv5[q].astype(F32)

    for h in range(2):
        rows = []
        for i in range(4):
            tile = chosen[64 * h + 16 * i : 64 * h + 16 * i + 16]
            other = pltpu.roll(tile, 64, 1)
            if i % 2 == 0:
                top, low = jnp.where(low_half, tile, 0.0), jnp.where(low_half, other, 0.0)
            else:
                top, low = jnp.where(low_half, 0.0, other), jnp.where(low_half, 0.0, tile)
            here = jnp.concatenate([top, low], axis=0)
            none = jnp.zeros_like(here)
            rows.append(jnp.concatenate([here, none] if i < 2 else [none, here], axis=1))
        lhs = jnp.concatenate(rows, axis=0).astype(BF16)
        deep = slice(256 * h, 256 * h + 256)
        for k in range(0, VIS, 256):
            re = jnp.dot(lhs, v_v[deep, k : k + 256], preferred_element_type=F32)
            im = jnp.dot(lhs, v_v[deep, VIS + k : VIS + k + 256], preferred_element_type=F32)
            for i in range(4):
                j = 4 * h + i
                a = (re[32 * i : 32 * i + 32], im[32 * i : 32 * i + 32])
                b = (u_v[0, j, :, k : k + 256], u_v[1, j, :, k : k + 256])
                vis = cmul(a, b)
                for part in range(2):
                    out_ref[0, 0, j, part : part + 1, k : k + 256] = jnp.sum(
                        vis[part], axis=0, keepdims=True
                    )

    @pl.loop(1, 8)
    def _(i):
        copy1((col + i) % 8).wait_send()
        copy_s((g_me + i) % 8, g_me).wait_send()
        copy2((col + i) % 8).wait_send()
        copy3((zg + i) % 8, zg).wait_send()

    @pl.when(col != g_me)
    def _():
        copy2(col).wait_send()

    @pl.loop(1, 16)
    def _(i):
        copy4((place + i) % 16, place).wait_send()

    @pl.loop(1, 4)
    def _(i):
        copy5((q_me + i) % 4, q_me).wait_send()


def shards(
    facet_strips, facet_offsets, column_offsets, row_offsets, tile_lists, tile_counts, uv_index
):
    smem = pl.BlockSpec(memory_space=pltpu.SMEM)
    anywhere = pl.BlockSpec(memory_space=pl.ANY)
    dma = pltpu.SemaphoreType.DMA
    return pl.pallas_call(
        kernel,
        out_shape=jax.ShapeDtypeStruct((1, 1, CAP, 2, VIS), F32),
        in_specs=[anywhere, smem, smem, smem, smem, smem, anywhere],
        out_specs=pl.BlockSpec(memory_space=pltpu.VMEM),
        scratch_shapes=[
            pltpu.VMEM((LEN, 2 * W), BF16),
            pltpu.VMEM((CAP, 2, VIS), I32),
            pltpu.VMEM((2 * S, LEN), BF16),
            pltpu.VMEM((8, 32, 2 * W), BF16),
            pltpu.VMEM((8, 32, 2 * W), BF16),
            pltpu.VMEM((32, 2 * W), BF16),
            pltpu.VMEM((8, 32, 2 * W), BF16),
            pltpu.VMEM((2 * W, 4 * S), BF16),
            pltpu.VMEM((8, 16, W), BF16),
            pltpu.VMEM((8, 16, W), BF16),
            pltpu.VMEM((16, 16, W), BF16),
            pltpu.VMEM((16, W), I32),
            pltpu.VMEM((8, 16, W), I32),
            pltpu.VMEM((4, W, 2 * W), BF16),
            pltpu.VMEM((4, W, W), BF16),
            pltpu.VMEM((4, W, W), BF16),
            pltpu.VMEM((2, 5, 2, CAP, VIS), F32),
            pltpu.VMEM((2, CAP, TILE, VIS), F32),
            pltpu.VMEM((CAP * 64, 2 * VIS), BF16),
            dma((3,)),
            dma((8,)),
            dma((8,)),
            dma((8,)),
            dma((8,)),
            dma((8,)),
            dma((8,)),
            dma((8,)),
            dma((8,)),
            dma((16,)),
            dma((16,)),
            dma((4,)),
            dma((4,)),
        ],
        compiler_params=pltpu.CompilerParams(
            collective_id=0, has_side_effects=True, vmem_limit_bytes=48 * 1024 * 1024
        ),
    )(facet_strips, facet_offsets, column_offsets, row_offsets, tile_lists, tile_counts, uv_index)


def solution(mesh):
    in_specs = (
        P("facet", None, "col", None),
        P("facet", None),
        P("col"),
        P(),
        P("col", "facet", None),
        P("col", "facet"),
        P("col", "facet", None, None, None),
    )
    out_specs = P("col", "facet", None, None, None)
    return jax.shard_map(shards, mesh=mesh, in_specs=in_specs, out_specs=out_specs, check_vma=False)
```

```python
import math

import jax
import jax.numpy as jnp
from jax import lax
from jax.experimental import pallas as pl
from jax.experimental.pallas import tpu as pltpu
from jax.sharding import PartitionSpec as P

L = 8192
W = 128
S = 256
TILE = 32
NTOT = 65536
UV_STEPS = 4096
VIS = 1024
CAP = 8
FACETS = 64
LEN = 1024
MESH = pl.DeviceIdType.MESH
FAR = ((1, 2), (1, 1), (1, 3), (0, 2), (1, 0), (0, 1), (0, 3))
F32 = jnp.float32
BF16 = jnp.bfloat16
I32 = jnp.int32


def unit(index):
    index = index & (NTOT - 1)
    index = jnp.where(index >= NTOT // 2, index - NTOT, index)
    angle = index.astype(F32) * (2.0 * math.pi / NTOT)
    return jnp.cos(angle), jnp.sin(angle)


def cmul(a, b):
    return a[0] * b[0] - a[1] * b[1], a[0] * b[1] + a[1] * b[0]


def iota(shape, dim):
    return lax.broadcasted_iota(I32, shape, dim)


def facet_of(x_hi, z, core):
    return (x_hi * 16 + z) * 2 + core


def group_facet(g, zg):
    return facet_of(g // 4, 2 * zg + g % 2, (g // 2) % 2)


def kernel(
    strip_ref,
    offsets_hbm,
    column_hbm,
    row_hbm,
    lists_hbm,
    counts_hbm,
    uv_ref,
    out_ref,
    offsets_ref,
    column_ref,
    row_ref,
    lists_ref,
    counts_ref,
    strip_v,
    uv_v,
    left_v,
    send1,
    recv1,
    block2,
    recv2,
    table_v,
    send3,
    recv3,
    recv4,
    small_v,
    recv_s,
    pick_v,
    send5,
    recv5,
    pow_v,
    u_v,
    v_v,
    load_sem,
    s_s,
    r_s,
    s_1,
    r_1,
    s_2,
    r_2,
    s_3,
    r_3,
    s_4,
    r_4,
    s_5,
    r_5,
):
    facet = lax.axis_index("facet")
    col = lax.axis_index("col")
    x_hi = facet // 32
    z = (facet // 2) % 16
    core = facet % 2
    zg = z // 2
    zp = z % 2
    q_me = x_hi * 2 + core
    g_me = q_me * 2 + zp

    loads = [
        pltpu.make_async_copy(strip_ref.at[0, 0], strip_v.at[:, pl.ds(0, W)], load_sem.at[0]),
        pltpu.make_async_copy(strip_ref.at[0, 1], strip_v.at[:, pl.ds(W, W)], load_sem.at[1]),
        pltpu.make_async_copy(uv_ref.at[0, 0], uv_v, load_sem.at[2]),
        pltpu.make_async_copy(offsets_hbm, offsets_ref, load_sem.at[3]),
        pltpu.make_async_copy(row_hbm, row_ref, load_sem.at[4]),
        pltpu.make_async_copy(column_hbm, column_ref, load_sem.at[5]),
        pltpu.make_async_copy(lists_hbm, lists_ref, load_sem.at[6]),
        pltpu.make_async_copy(counts_hbm, counts_ref, load_sem.at[7]),
    ]
    for n in (3, 4, 0, 1, 5, 6, 7, 2):
        loads[n].start()

    barrier = pltpu.get_barrier_semaphore()

    def greet(f, c):
        pl.semaphore_signal(barrier, inc=1, device_id=(f, c), device_id_type=MESH)

    for i in (4, 3, 5, 2, 6, 1, 7):
        greet(facet_of(x_hi, (z + 2 * i) % 16, core), col)
    for i in (3, 13):
        greet(facet_of(x_hi, (z + i) % 16, core), col)
    greet(facet_of(x_hi, (z + 2 * zp + 15) % 16, core), col)

    @pl.loop(1, 8)
    def _(i):
        greet(facet, (col + i) % 8)

    @pl.loop(1, 8)
    def _(i):
        greet(group_facet((g_me + i) % 8, zg), col)

    @pl.when(col != g_me)
    def _():
        @pl.loop(0, 8)
        def _(g):
            greet(group_facet(g, zg), g_me)

    loads[3].wait()
    loads[4].wait()

    row0 = row_ref[0]
    cells = offsets_ref[0, 0] + col * LEN + iota((8, LEN), 1)
    base = unit((row0 + 8 * iota((8, LEN), 0)) * cells)
    scale = 1.0 / math.sqrt(L)
    step = unit(64 * cells)

    def left_body(t, value):
        nxt = cmul(value, step)
        at = pl.ds(pl.multiple_of(16 * t, 16), 16)
        left_v[at, :] = jnp.concatenate([value[0], nxt[0]], axis=0).astype(BF16)
        at = pl.ds(pl.multiple_of(S + 16 * t, 16), 16)
        left_v[at, :] = jnp.concatenate([value[1], nxt[1]], axis=0).astype(BF16)
        return cmul(nxt, step)

    lax.fori_loop(0, 16, left_body, (base[0] * scale, base[1] * scale))

    loads[0].wait()
    loads[1].wait()
    both = jnp.dot(left_v[...], strip_v[...], preferred_element_type=F32)
    real = both[:S, :W] + both[S:, W:]
    imag = both[:S, W:] - both[S:, :W]
    send1[...] = jnp.concatenate([real, imag], axis=1).astype(BF16).reshape(8, 32, 2 * W)

    pl.semaphore_wait(barrier, 31)

    def copy1(c):
        return pltpu.make_async_remote_copy(
            src_ref=send1.at[c], dst_ref=recv1.at[col], send_sem=s_1.at[c], recv_sem=r_1.at[col],
            device_id=(facet, c), device_id_type=MESH,
        )

    def from1(c):
        return pltpu.make_async_remote_copy(
            src_ref=send1.at[c], dst_ref=recv1.at[c], send_sem=s_1.at[c], recv_sem=r_1.at[c],
            device_id=(facet, c), device_id_type=MESH,
        )

    x_lo = col // 4
    y = col % 4

    def col_at(far):
        return (x_lo + far[0]) % 2 * 4 + (y + far[1]) % 4

    for far in FAR:
        copy1(col_at(far)).start()

    recv1[pl.ds(col, 1)] = send1[pl.ds(col, 1)]

    loads[6].wait()
    loads[7].wait()
    lanes = iota((8, W), 0)
    ids = jnp.full((8, W), -1, I32)
    for j in range(CAP):
        ids = jnp.where((lanes == j) & (j < counts_ref[0, 0]), lists_ref[0, 0, j], ids)
    small_v[0:8, :] = ids
    small_v[8:16, :] = jnp.full((8, W), offsets_ref[0, 1], I32)
    recv_s[pl.ds(g_me, 1)] = small_v[...][None]

    def copy_s(g, dst):
        return pltpu.make_async_remote_copy(
            src_ref=small_v, dst_ref=recv_s.at[dst], send_sem=s_s.at[g], recv_sem=r_s.at[dst],
            device_id=(group_facet(g, zg), col), device_id_type=MESH,
        )

    @pl.loop(1, 8)
    def _(i):
        copy_s((g_me + i) % 8, g_me).start()

    loads[5].wait()
    lane = iota((8, 2 * S), 1)
    sample = column_ref[0] + 256 * (32 * (lane // 64) + lane % 32)
    quarter = (NTOT // 4) * ((lane // 32) % 2)
    base_r = unit(iota((8, 2 * S), 0) * sample + quarter)
    step_r = unit(8 * sample)

    def right_body(t, value):
        nxt = cmul(value, step_r)
        re = jnp.concatenate([value[0], nxt[0]], axis=0)
        im = jnp.concatenate([value[1], nxt[1]], axis=0)
        top = pl.ds(pl.multiple_of(16 * t, 16), 16)
        low = pl.ds(pl.multiple_of(W + 16 * t, 16), 16)
        table_v[top, 0 : 2 * S] = re.astype(BF16)
        table_v[low, 0 : 2 * S] = im.astype(BF16)
        table_v[top, 2 * S :] = (-im).astype(BF16)
        table_v[low, 2 * S :] = re.astype(BF16)
        return cmul(nxt, step_r)

    lax.fori_loop(0, 8, right_body, base_r)

    @pl.loop(1, 8)
    def _(i):
        from1((col + i) % 8).wait_recv()

    total = recv1[0].astype(F32)
    for c in range(1, 8):
        total = total + recv1[c].astype(F32)
    block2[...] = total.astype(BF16)

    def copy2(c):
        return pltpu.make_async_remote_copy(
            src_ref=block2, dst_ref=recv2.at[g_me], send_sem=s_2.at[c], recv_sem=r_2.at[g_me],
            device_id=(group_facet(col, zg), c), device_id_type=MESH,
        )

    def from2(g):
        return pltpu.make_async_remote_copy(
            src_ref=block2, dst_ref=recv2.at[g], send_sem=s_2.at[g], recv_sem=r_2.at[g],
            device_id=(group_facet(g, zg), g_me), device_id_type=MESH,
        )

    @pl.when(col == g_me)
    def _():
        recv2[pl.ds(g_me, 1)] = block2[...][None]

    @pl.when(col != g_me)
    def _():
        copy2(col).start()

    for far in FAR:
        copy2(col_at(far)).start()

    loads[2].wait()
    for part in range(2):
        index = jnp.concatenate([uv_v[j, part : part + 1, :] for j in range(CAP)], axis=0)
        value = unit(index * (NTOT // UV_STEPS))
        for k in range(5):
            pow_v[part, k, 0] = value[0]
            pow_v[part, k, 1] = value[1]
            value = cmul(value, value)

    sub = iota((8, VIS), 0)

    def powers(part, j):
        def power(k):
            return tuple(
                jnp.broadcast_to(pow_v[part, k, h, pl.ds(j, 1), :], (8, VIS)) for h in range(2)
            )

        def chosen_power(k):
            re, im = power(k)
            on = (sub & (1 << k)) != 0
            return jnp.where(on, re, 1.0), jnp.where(on, im, 0.0)

        low = cmul(cmul(chosen_power(0), chosen_power(1)), chosen_power(2))
        sixteen = power(4)
        second = cmul(low, power(3))
        third = cmul(low, sixteen)
        fourth = cmul(second, sixteen)
        parts = (low, second, third, fourth)
        return tuple(jnp.concatenate([p[h] for p in parts], axis=0) for h in range(2))

    @pl.loop(0, CAP)
    def _(j):
        re, im = powers(0, j)
        u_v[0, j] = re * (1.0 / TILE)
        u_v[1, j] = im * (1.0 / TILE)
        re, im = powers(1, j)
        top = pl.ds(pl.multiple_of(64 * j, 32), 32)
        low = pl.ds(pl.multiple_of(64 * j + 32, 32), 32)
        v_v[top, 0:VIS] = re.astype(BF16)
        v_v[top, VIS:] = im.astype(BF16)
        v_v[low, 0:VIS] = (-im).astype(BF16)
        v_v[low, VIS:] = re.astype(BF16)

    @pl.loop(1, 8)
    def _(i):
        copy_s((g_me + i) % 8, (g_me + i) % 8).wait_recv()

    across = jnp.zeros((8, W), I32)
    for g in range(8):
        across = jnp.where(lanes == g, recv_s[g, 8:16, :], across)
    across = jnp.concatenate([across] * 4, axis=1)
    turn = unit(across * sample)
    norm = 1.0 / math.sqrt(W * FACETS)
    turn = (turn[0] * norm, turn[1] * norm)

    entry = iota((16, 2 * W), 1)
    diagonal = iota((16, 2 * W), 0) == entry % 16
    entry = entry // 16
    entry = 16 * q_me + 8 * (entry // 2 % 2) + entry // 4 + 4 * (entry % 2)

    @pl.loop(0, 4)
    def _(q):
        for j in range(CAP):
            wanted = recv_s[2 * q + zp, j : j + 1, :]
            wanted = jnp.broadcast_to(jnp.concatenate([wanted, wanted], axis=1), (16, 2 * W))
            pick = jnp.where((wanted == entry) & diagonal, 1.0, 0.0)
            pick_v[q, 16 * j : 16 * j + 16, :] = pick.astype(BF16)

    @pl.when(col == g_me)
    def _():
        @pl.loop(1, 8)
        def _(i):
            from2((g_me + i) % 8).wait_recv()

    @pl.when(col != g_me)
    def _():
        @pl.loop(0, 8)
        def _(g):
            from2(g).wait_recv()

    grid = jnp.dot(
        recv2[...].reshape(8 * 32, 2 * W), table_v[...], preferred_element_type=F32
    )
    terms = None
    for g in range(8):
        rows = grid[32 * g : 32 * g + 32]
        term = rows[:, : 2 * S] * turn[0][g : g + 1] + rows[:, 2 * S :] * turn[1][g : g + 1]
        terms = term if terms is None else terms + term

    low_half = iota((16, W), 1) < 64
    for v in range(4):
        top = terms[0:16, W * v : W * v + W]
        low = terms[16:32, W * v : W * v + W]
        send3[2 * v % 4, v // 2] = jnp.where(low_half, top, pltpu.roll(low, 64, 1)).astype(BF16)
        send3[(2 * v + 1) % 4, v // 2] = jnp.where(low_half, pltpu.roll(top, 64, 1), low).astype(BF16)

    def copy3(n, dst):
        return pltpu.make_async_remote_copy(
            src_ref=send3.at[n % 4], dst_ref=recv3.at[dst], send_sem=s_3.at[n], recv_sem=r_3.at[dst],
            device_id=(facet_of(x_hi, 2 * n + zp, core), col), device_id_type=MESH,
        )

    for i in (4, 3, 5, 2, 6, 1, 7):
        copy3((zg + i) % 8, zg).start()

    recv3[pl.ds(zg, 1)] = send3[pl.ds(zg % 4, 1)]

    @pl.loop(1, 8)
    def _(i):
        copy3((zg + i) % 8, (zg + i) % 8).wait_recv()

    total = recv3[0].astype(F32)
    for b in range(1, 8):
        total = total + recv3[b].astype(F32)
    place = z % 8
    recv4[pl.ds(place, 1)] = total.astype(BF16)[None]

    def copy4(i, dst):
        return pltpu.make_async_remote_copy(
            src_ref=recv4.at[place], dst_ref=recv4.at[dst], send_sem=s_4.at[dst], recv_sem=r_4.at[dst],
            device_id=(facet_of(x_hi, (z + i) % 16, core), col), device_id_type=MESH,
        )

    def send4(i):
        return pltpu.make_async_remote_copy(
            src_ref=recv4.at[place], dst_ref=recv4.at[place],
            send_sem=s_4.at[(place + i) % 8], recv_sem=r_4.at[place],
            device_id=(facet_of(x_hi, (z + i) % 16, core), col), device_id_type=MESH,
        )

    for i in (4, 13, 3, 14, 2, 15, 1):
        send4(i).start()

    @pl.loop(1, 8)
    def _(i):
        copy4(i, (place + i) % 8).wait_recv()

    picks = jnp.dot(
        pick_v[...].reshape(4 * W, 2 * W), recv4[...].reshape(2 * W, W), preferred_element_type=F32
    )
    send5[...] = picks.astype(BF16).reshape(4, W, W)

    def copy5(q, dst):
        return pltpu.make_async_remote_copy(
            src_ref=send5.at[q], dst_ref=recv5.at[dst], send_sem=s_5.at[q], recv_sem=r_5.at[dst],
            device_id=(facet_of(q // 2, z, q % 2), col), device_id_type=MESH,
        )

    @pl.loop(1, 4)
    def _(i):
        copy5((q_me + i) % 4, q_me).start()

    recv5[pl.ds(q_me, 1)] = send5[pl.ds(q_me, 1)]

    @pl.loop(1, 4)
    def _(i):
        copy5((q_me + i) % 4, (q_me + i) % 4).wait_recv()

    chosen = recv5[0].astype(F32)
    for q in range(1, 4):
        chosen = chosen + recv5[q].astype(F32)

    for h in range(2):
        rows = []
        for i in range(4):
            tile = chosen[64 * h + 16 * i : 64 * h + 16 * i + 16]
            other = pltpu.roll(tile, 64, 1)
            if i % 2 == 0:
                top, low = jnp.where(low_half, tile, 0.0), jnp.where(low_half, other, 0.0)
            else:
                top, low = jnp.where(low_half, 0.0, other), jnp.where(low_half, 0.0, tile)
            here = jnp.concatenate([top, low], axis=0)
            none = jnp.zeros_like(here)
            rows.append(jnp.concatenate([here, none] if i < 2 else [none, here], axis=1))
        lhs = jnp.concatenate(rows, axis=0).astype(BF16)
        deep = slice(256 * h, 256 * h + 256)
        for k in range(0, VIS, 256):
            re = jnp.dot(lhs, v_v[deep, k : k + 256], preferred_element_type=F32)
            im = jnp.dot(lhs, v_v[deep, VIS + k : VIS + k + 256], preferred_element_type=F32)
            for i in range(4):
                j = 4 * h + i
                a = (re[32 * i : 32 * i + 32], im[32 * i : 32 * i + 32])
                b = (u_v[0, j, :, k : k + 256], u_v[1, j, :, k : k + 256])
                vis = cmul(a, b)
                for part in range(2):
                    out_ref[0, 0, j, part : part + 1, k : k + 256] = jnp.sum(
                        vis[part], axis=0, keepdims=True
                    )

    @pl.loop(1, 8)
    def _(i):
        copy1((col + i) % 8).wait_send()
        copy_s((g_me + i) % 8, g_me).wait_send()
        copy2((col + i) % 8).wait_send()
        copy3((zg + i) % 8, zg).wait_send()

    @pl.when(col != g_me)
    def _():
        copy2(col).wait_send()

    @pl.loop(1, 8)
    def _(i):
        send4(i).wait_send()

    @pl.loop(1, 4)
    def _(i):
        copy5((q_me + i) % 4, q_me).wait_send()


def shards(
    facet_strips, facet_offsets, column_offsets, row_offsets, tile_lists, tile_counts, uv_index
):
    anywhere = pl.BlockSpec(memory_space=pl.ANY)
    dma = pltpu.SemaphoreType.DMA
    return pl.pallas_call(
        kernel,
        out_shape=jax.ShapeDtypeStruct((1, 1, CAP, 2, VIS), F32),
        in_specs=[anywhere] * 7,
        out_specs=pl.BlockSpec(memory_space=pltpu.VMEM),
        scratch_shapes=[
            pltpu.SMEM((1, 2), I32),
            pltpu.SMEM((1,), I32),
            pltpu.SMEM((1,), I32),
            pltpu.SMEM((1, 1, CAP), I32),
            pltpu.SMEM((1, 1), I32),
            pltpu.VMEM((LEN, 2 * W), BF16),
            pltpu.VMEM((CAP, 2, VIS), I32),
            pltpu.VMEM((2 * S, LEN), BF16),
            pltpu.VMEM((8, 32, 2 * W), BF16),
            pltpu.VMEM((8, 32, 2 * W), BF16),
            pltpu.VMEM((32, 2 * W), BF16),
            pltpu.VMEM((8, 32, 2 * W), BF16),
            pltpu.VMEM((2 * W, 4 * S), BF16),
            pltpu.VMEM((4, 2, 16, W), BF16),
            pltpu.VMEM((8, 2, 16, W), BF16),
            pltpu.VMEM((8, 2, 16, W), BF16),
            pltpu.VMEM((16, W), I32),
            pltpu.VMEM((8, 16, W), I32),
            pltpu.VMEM((4, W, 2 * W), BF16),
            pltpu.VMEM((4, W, W), BF16),
            pltpu.VMEM((4, W, W), BF16),
            pltpu.VMEM((2, 5, 2, CAP, VIS), F32),
            pltpu.VMEM((2, CAP, TILE, VIS), F32),
            pltpu.VMEM((CAP * 64, 2 * VIS), BF16),
            dma((8,)),
            dma((8,)),
            dma((8,)),
            dma((8,)),
            dma((8,)),
            dma((8,)),
            dma((8,)),
            dma((8,)),
            dma((8,)),
            dma((8,)),
            dma((8,)),
            dma((4,)),
            dma((4,)),
        ],
        compiler_params=pltpu.CompilerParams(
            collective_id=0, has_side_effects=True, vmem_limit_bytes=63 * 1024 * 1024
        ),
    )(facet_strips, facet_offsets, column_offsets, row_offsets, tile_lists, tile_counts, uv_index)


def solution(mesh):
    in_specs = (
        P("facet", None, "col", None),
        P("facet", None),
        P("col"),
        P(),
        P("col", "facet", None),
        P("col", "facet"),
        P("col", "facet", None, None, None),
    )
    out_specs = P("col", "facet", None, None, None)
    return jax.shard_map(shards, mesh=mesh, in_specs=in_specs, out_specs=out_specs, check_vma=False)
```

```python
import math

import jax
import jax.numpy as jnp
from jax import lax
from jax.experimental import pallas as pl
from jax.experimental.pallas import tpu as pltpu
from jax.sharding import PartitionSpec as P

L = 8192
W = 128
S = 256
TILE = 32
NTOT = 65536
UV_STEPS = 4096
VIS = 1024
CAP = 8
FACETS = 64
LEN = 1024
MESH = pl.DeviceIdType.MESH
DEAL = 0
ORDER2 = ((0, 2), (0, 1), (0, 3), (1, 2), (0, 0), (1, 1), (1, 3), (1, 0))
AROUND = (4, -3, 3, -2, 2, -1, 1, 0)
FAR = ((1, 2), (1, 1), (1, 3), (0, 2), (1, 0), (0, 1), (0, 3))
F32 = jnp.float32
BF16 = jnp.bfloat16
I32 = jnp.int32


def unit(index):
    index = index & (NTOT - 1)
    index = jnp.where(index >= NTOT // 2, index - NTOT, index)
    angle = index.astype(F32) * (2.0 * math.pi / NTOT)
    return jnp.cos(angle), jnp.sin(angle)


def cmul(a, b):
    return a[0] * b[0] - a[1] * b[1], a[0] * b[1] + a[1] * b[0]


def iota(shape, dim):
    return lax.broadcasted_iota(I32, shape, dim)


def facet_of(x_hi, z, core):
    return (x_hi * 16 + z) * 2 + core


def group_facet(g, zg):
    return facet_of(g // 4, 2 * zg + g % 2, (g // 2) % 2)


def kernel(
    strip_ref,
    offsets_hbm,
    column_hbm,
    row_hbm,
    lists_hbm,
    counts_hbm,
    uv_ref,
    out_ref,
    offsets_ref,
    column_ref,
    row_ref,
    lists_ref,
    counts_ref,
    strip_v,
    uv_v,
    left_v,
    send1,
    recv1,
    block2,
    recv2,
    table_v,
    send3,
    recv3,
    recv4,
    small_v,
    recv_s,
    ids_v,
    recv_i,
    pick_v,
    send5,
    recv5,
    pow_v,
    u_v,
    v_v,
    load_sem,
    s_s,
    r_s,
    s_i,
    r_i,
    s_1,
    r_1,
    s_2,
    r_2,
    s_3,
    r_3,
    s_4,
    r_4,
    s_5,
    r_5,
):
    facet = lax.axis_index("facet")
    col = lax.axis_index("col")
    x_hi = facet // 32
    z = (facet // 2) % 16
    core = facet % 2
    zg = z // 2
    zp = z % 2
    q_me = x_hi * 2 + core
    g_me = q_me * 2 + zp
    x_lo = col // 4
    y = col % 4

    def block_of(c, x):
        return (c // 4 + x + DEAL) % 2 * 4 + c % 4

    def col_of(block, x):
        return (block // 4 + x + DEAL) % 2 * 4 + block % 4

    target = block_of(col, x_hi)

    loads = [
        pltpu.make_async_copy(strip_ref.at[0, 0], strip_v.at[:, pl.ds(0, W)], load_sem.at[0]),
        pltpu.make_async_copy(strip_ref.at[0, 1], strip_v.at[:, pl.ds(W, W)], load_sem.at[1]),
        pltpu.make_async_copy(uv_ref.at[0, 0], uv_v, load_sem.at[2]),
        pltpu.make_async_copy(offsets_hbm, offsets_ref, load_sem.at[3]),
        pltpu.make_async_copy(row_hbm, row_ref, load_sem.at[4]),
        pltpu.make_async_copy(column_hbm, column_ref, load_sem.at[5]),
        pltpu.make_async_copy(lists_hbm, lists_ref, load_sem.at[6]),
        pltpu.make_async_copy(counts_hbm, counts_ref, load_sem.at[7]),
    ]
    for n in (3, 4, 0, 1, 5, 6, 7, 2):
        loads[n].start()

    barrier = pltpu.get_barrier_semaphore()

    def greet(f, c):
        pl.semaphore_signal(barrier, inc=1, device_id=(f, c), device_id_type=MESH)

    for i in (4, 3, 5, 2, 6, 1, 7):
        greet(facet_of(x_hi, (z + 2 * i) % 16, core), col)
    for i in (3, 13):
        greet(facet_of(x_hi, (z + i) % 16, core), col)
    greet(facet_of(x_hi, (z + 2 * zp + 15) % 16, core), col)
    for i in (-4, 3, -3, 2, -2, 2 * zp - 1):
        greet(facet_of(1 - x_hi, (z + 16 + i) % 16, core), col)

    @pl.loop(1, 8)
    def _(i):
        greet(facet, (col + i) % 8)

    @pl.loop(1, 8)
    def _(i):
        greet(group_facet((g_me + i) % 8, zg), col)

    @pl.loop(0, 8)
    def _(g):
        source = col_of(g_me, g // 4)

        @pl.when(source != col)
        def _():
            greet(group_facet(g, zg), source)

    loads[3].wait()
    loads[4].wait()

    row0 = row_ref[0]
    cells = offsets_ref[0, 0] + col * LEN + iota((8, LEN), 1)
    base = unit((row0 + 8 * iota((8, LEN), 0)) * cells)
    scale = 1.0 / math.sqrt(L)
    step = unit(64 * cells)

    def left_body(t, value):
        nxt = cmul(value, step)
        at = pl.ds(pl.multiple_of(16 * t, 16), 16)
        left_v[at, :] = jnp.concatenate([value[0], nxt[0]], axis=0).astype(BF16)
        at = pl.ds(pl.multiple_of(S + 16 * t, 16), 16)
        left_v[at, :] = jnp.concatenate([value[1], nxt[1]], axis=0).astype(BF16)
        return cmul(nxt, step)

    lax.fori_loop(0, 16, left_body, (base[0] * scale, base[1] * scale))

    loads[0].wait()
    loads[1].wait()
    both = jnp.dot(left_v[...], strip_v[...], preferred_element_type=F32)
    real = both[:S, :W] + both[S:, W:]
    imag = both[:S, W:] - both[S:, :W]
    send1[...] = jnp.concatenate([real, imag], axis=1).astype(BF16).reshape(8, 32, 2 * W)

    pl.semaphore_wait(barrier, 37)

    def copy1(c):
        return pltpu.make_async_remote_copy(
            src_ref=send1.at[block_of(c, x_hi)], dst_ref=recv1.at[col], send_sem=s_1.at[c], recv_sem=r_1.at[col],
            device_id=(facet, c), device_id_type=MESH,
        )

    def from1(c):
        return pltpu.make_async_remote_copy(
            src_ref=send1.at[block_of(c, x_hi)], dst_ref=recv1.at[c], send_sem=s_1.at[c], recv_sem=r_1.at[c],
            device_id=(facet, c), device_id_type=MESH,
        )

    def col_at(far):
        return (x_lo + far[0]) % 2 * 4 + (y + far[1]) % 4

    for far in FAR:
        copy1(col_at(far)).start()

    recv1[pl.ds(col, 1)] = send1[pl.ds(target, 1)]

    loads[6].wait()
    loads[7].wait()
    lanes = iota((8, W), 0)
    ids = jnp.full((8, W), -1, I32)
    for j in range(CAP):
        ids = jnp.where((lanes == j) & (j < counts_ref[0, 0]), lists_ref[0, 0, j], ids)
    ids_v[...] = ids
    small_v[...] = jnp.full((8, W), offsets_ref[0, 1], I32)
    recv_s[pl.ds(g_me, 1)] = small_v[...][None]

    def copy_s(g, dst):
        return pltpu.make_async_remote_copy(
            src_ref=small_v, dst_ref=recv_s.at[dst], send_sem=s_s.at[g], recv_sem=r_s.at[dst],
            device_id=(group_facet(g, zg), col), device_id_type=MESH,
        )

    copy_i = pltpu.make_async_remote_copy(
        src_ref=ids_v, dst_ref=recv_i, send_sem=s_i, recv_sem=r_i,
        device_id=(facet_of(x_hi, z, 1 - core), col), device_id_type=MESH,
    )
    copy_i.start()

    @pl.loop(1, 8)
    def _(i):
        copy_s((g_me + i) % 8, g_me).start()

    loads[5].wait()
    lane = iota((8, 2 * S), 1)
    sample = column_ref[0] + 256 * (32 * (lane // 64) + lane % 32)
    quarter = (NTOT // 4) * ((lane // 32) % 2)
    base_r = unit(iota((8, 2 * S), 0) * sample + quarter)
    step_r = unit(8 * sample)

    def right_body(t, value):
        nxt = cmul(value, step_r)
        re = jnp.concatenate([value[0], nxt[0]], axis=0)
        im = jnp.concatenate([value[1], nxt[1]], axis=0)
        top = pl.ds(pl.multiple_of(16 * t, 16), 16)
        low = pl.ds(pl.multiple_of(W + 16 * t, 16), 16)
        table_v[top, 0 : 2 * S] = re.astype(BF16)
        table_v[low, 0 : 2 * S] = im.astype(BF16)
        table_v[top, 2 * S :] = (-im).astype(BF16)
        table_v[low, 2 * S :] = re.astype(BF16)
        return cmul(nxt, step_r)

    lax.fori_loop(0, 8, right_body, base_r)

    @pl.loop(1, 8)
    def _(i):
        from1((col + i) % 8).wait_recv()

    total = recv1[0].astype(F32)
    for c in range(1, 8):
        total = total + recv1[c].astype(F32)
    block2[...] = total.astype(BF16)

    def copy2(c):
        return pltpu.make_async_remote_copy(
            src_ref=block2, dst_ref=recv2.at[g_me], send_sem=s_2.at[c], recv_sem=r_2.at[g_me],
            device_id=(group_facet(target, zg), c), device_id_type=MESH,
        )

    def from2(g):
        return pltpu.make_async_remote_copy(
            src_ref=block2, dst_ref=recv2.at[g], send_sem=s_2.at[g], recv_sem=r_2.at[g],
            device_id=(group_facet(g, zg), col_of(g_me, g // 4)), device_id_type=MESH,
        )

    for x, dy in ORDER2:
        c = 4 * x + (y + dy) % 4

        @pl.when((target != g_me) | (c != col))
        def _():
            copy2(c).start()

    @pl.when(target == g_me)
    def _():
        recv2[pl.ds(g_me, 1)] = block2[...][None]

    loads[2].wait()
    for part in range(2):
        index = jnp.concatenate([uv_v[j, part : part + 1, :] for j in range(CAP)], axis=0)
        value = unit(index * (NTOT // UV_STEPS))
        for k in range(5):
            pow_v[part, k, 0] = value[0]
            pow_v[part, k, 1] = value[1]
            value = cmul(value, value)

    sub = iota((8, VIS), 0)

    def powers(part, j):
        def power(k):
            return tuple(
                jnp.broadcast_to(pow_v[part, k, h, pl.ds(j, 1), :], (8, VIS)) for h in range(2)
            )

        def chosen_power(k):
            re, im = power(k)
            on = (sub & (1 << k)) != 0
            return jnp.where(on, re, 1.0), jnp.where(on, im, 0.0)

        low = cmul(cmul(chosen_power(0), chosen_power(1)), chosen_power(2))
        sixteen = power(4)
        second = cmul(low, power(3))
        third = cmul(low, sixteen)
        fourth = cmul(second, sixteen)
        parts = (low, second, third, fourth)
        return tuple(jnp.concatenate([p[h] for p in parts], axis=0) for h in range(2))

    @pl.loop(0, CAP)
    def _(j):
        re, im = powers(0, j)
        u_v[0, j] = re * (1.0 / TILE)
        u_v[1, j] = im * (1.0 / TILE)
        re, im = powers(1, j)
        top = pl.ds(pl.multiple_of(64 * j, 32), 32)
        low = pl.ds(pl.multiple_of(64 * j + 32, 32), 32)
        v_v[top, 0:VIS] = re.astype(BF16)
        v_v[top, VIS:] = im.astype(BF16)
        v_v[low, 0:VIS] = (-im).astype(BF16)
        v_v[low, VIS:] = re.astype(BF16)

    @pl.loop(1, 8)
    def _(i):
        copy_s((g_me + i) % 8, (g_me + i) % 8).wait_recv()

    across = jnp.zeros((8, W), I32)
    for g in range(8):
        across = jnp.where(lanes == g, recv_s[g], across)
    across = jnp.concatenate([across] * 4, axis=1)
    turn = unit(across * sample)
    norm = 1.0 / math.sqrt(W * FACETS)
    turn = (turn[0] * norm, turn[1] * norm)

    copy_i.wait_recv()
    entry = iota((16, 4 * W), 1)
    diagonal = iota((16, 4 * W), 0) == entry % 16
    entry = entry // 16
    at_place = entry // 2 % 8
    entry = 32 * (entry // 16) + 16 * core + 8 * (at_place % 2) + at_place // 2 + 4 * (entry % 2)
    for n, wanted_ref in enumerate((ids_v, recv_i)):
        for j in range(CAP):
            wanted = jnp.concatenate([wanted_ref[j : j + 1, :]] * 4, axis=1)
            pick = jnp.where((jnp.broadcast_to(wanted, entry.shape) == entry) & diagonal, 1.0, 0.0)
            pick_v[W * n + 16 * j : W * n + 16 * j + 16, :] = pick.astype(BF16)

    @pl.loop(0, 8)
    def _(g):
        @pl.when((target != g_me) | (g != g_me))
        def _():
            from2(g).wait_recv()

    grid = jnp.dot(
        recv2[...].reshape(8 * 32, 2 * W), table_v[...], preferred_element_type=F32
    )
    terms = None
    for g in range(8):
        rows = grid[32 * g : 32 * g + 32]
        term = rows[:, : 2 * S] * turn[0][g : g + 1] + rows[:, 2 * S :] * turn[1][g : g + 1]
        terms = term if terms is None else terms + term

    low_half = iota((16, W), 1) < 64
    for v in range(4):
        top = terms[0:16, W * v : W * v + W]
        low = terms[16:32, W * v : W * v + W]
        send3[2 * v % 4, v // 2] = jnp.where(low_half, top, pltpu.roll(low, 64, 1)).astype(BF16)
        send3[(2 * v + 1) % 4, v // 2] = jnp.where(low_half, pltpu.roll(top, 64, 1), low).astype(BF16)

    def copy3(n, dst):
        return pltpu.make_async_remote_copy(
            src_ref=send3.at[n % 4], dst_ref=recv3.at[dst], send_sem=s_3.at[n], recv_sem=r_3.at[dst],
            device_id=(facet_of(x_hi, 2 * n + zp, core), col), device_id_type=MESH,
        )

    for i in (4, 3, 5, 2, 6, 1, 7):
        copy3((zg + i) % 8, zg).start()

    recv3[pl.ds(zg, 1)] = send3[pl.ds(zg % 4, 1)]

    @pl.loop(1, 8)
    def _(i):
        copy3((zg + i) % 8, (zg + i) % 8).wait_recv()

    total = recv3[0].astype(F32)
    for b in range(1, 8):
        total = total + recv3[b].astype(F32)
    place = z % 8
    mine = 8 * x_hi + place
    recv4[pl.ds(mine, 1)] = total.astype(BF16)[None]

    def copy4(x, i, dst):
        there = 8 * x + (place + i) % 8
        return pltpu.make_async_remote_copy(
            src_ref=recv4.at[mine], dst_ref=recv4.at[dst], send_sem=s_4.at[there], recv_sem=r_4.at[dst],
            device_id=(facet_of(x, (z + i) % 16, core), col), device_id_type=MESH,
        )

    for i in AROUND:
        copy4(1 - x_hi, i + 16, mine).start()
    for i in AROUND[:-1]:
        copy4(x_hi, i + 16, mine).start()

    @pl.loop(1, 16)
    def _(i):
        n = (mine + i) % 16
        copy4(n // 8, n % 8 - place + 16, n).wait_recv()

    picks = jnp.dot(pick_v[...], recv4[...].reshape(4 * W, W), preferred_element_type=F32)
    send5[...] = picks.astype(BF16).reshape(2, W, W)
    copy5 = pltpu.make_async_remote_copy(
        src_ref=send5.at[1], dst_ref=recv5, send_sem=s_5, recv_sem=r_5,
        device_id=(facet_of(x_hi, z, 1 - core), col), device_id_type=MESH,
    )
    copy5.start()
    copy5.wait_recv()
    chosen = send5[0].astype(F32) + recv5[...].astype(F32)

    for h in range(2):
        rows = []
        for i in range(4):
            tile = chosen[64 * h + 16 * i : 64 * h + 16 * i + 16]
            other = pltpu.roll(tile, 64, 1)
            if i % 2 == 0:
                top, low = jnp.where(low_half, tile, 0.0), jnp.where(low_half, other, 0.0)
            else:
                top, low = jnp.where(low_half, 0.0, other), jnp.where(low_half, 0.0, tile)
            here = jnp.concatenate([top, low], axis=0)
            none = jnp.zeros_like(here)
            rows.append(jnp.concatenate([here, none] if i < 2 else [none, here], axis=1))
        lhs = jnp.concatenate(rows, axis=0).astype(BF16)
        deep = slice(256 * h, 256 * h + 256)
        for k in range(0, VIS, 256):
            re = jnp.dot(lhs, v_v[deep, k : k + 256], preferred_element_type=F32)
            im = jnp.dot(lhs, v_v[deep, VIS + k : VIS + k + 256], preferred_element_type=F32)
            for i in range(4):
                j = 4 * h + i
                a = (re[32 * i : 32 * i + 32], im[32 * i : 32 * i + 32])
                b = (u_v[0, j, :, k : k + 256], u_v[1, j, :, k : k + 256])
                vis = cmul(a, b)
                for part in range(2):
                    out_ref[0, 0, j, part : part + 1, k : k + 256] = jnp.sum(
                        vis[part], axis=0, keepdims=True
                    )

    @pl.loop(1, 8)
    def _(i):
        copy1((col + i) % 8).wait_send()
        copy_s((g_me + i) % 8, g_me).wait_send()
        copy3((zg + i) % 8, zg).wait_send()

    copy_i.wait_send()

    @pl.loop(0, 8)
    def _(c):
        @pl.when((target != g_me) | (c != col))
        def _():
            copy2(c).wait_send()

    @pl.loop(1, 16)
    def _(i):
        n = (mine + i) % 16
        copy4(n // 8, n % 8 - place + 16, mine).wait_send()

    copy5.wait_send()


def shards(
    facet_strips, facet_offsets, column_offsets, row_offsets, tile_lists, tile_counts, uv_index
):
    anywhere = pl.BlockSpec(memory_space=pl.ANY)
    dma = pltpu.SemaphoreType.DMA
    return pl.pallas_call(
        kernel,
        out_shape=jax.ShapeDtypeStruct((1, 1, CAP, 2, VIS), F32),
        in_specs=[anywhere] * 7,
        out_specs=pl.BlockSpec(memory_space=pltpu.VMEM),
        scratch_shapes=[
            pltpu.SMEM((1, 2), I32),
            pltpu.SMEM((1,), I32),
            pltpu.SMEM((1,), I32),
            pltpu.SMEM((1, 1, CAP), I32),
            pltpu.SMEM((1, 1), I32),
            pltpu.VMEM((LEN, 2 * W), BF16),
            pltpu.VMEM((CAP, 2, VIS), I32),
            pltpu.VMEM((2 * S, LEN), BF16),
            pltpu.VMEM((8, 32, 2 * W), BF16),
            pltpu.VMEM((8, 32, 2 * W), BF16),
            pltpu.VMEM((32, 2 * W), BF16),
            pltpu.VMEM((8, 32, 2 * W), BF16),
            pltpu.VMEM((2 * W, 4 * S), BF16),
            pltpu.VMEM((4, 2, 16, W), BF16),
            pltpu.VMEM((8, 2, 16, W), BF16),
            pltpu.VMEM((16, 2, 16, W), BF16),
            pltpu.VMEM((8, W), I32),
            pltpu.VMEM((8, 8, W), I32),
            pltpu.VMEM((8, W), I32),
            pltpu.VMEM((8, W), I32),
            pltpu.VMEM((2 * W, 4 * W), BF16),
            pltpu.VMEM((2, W, W), BF16),
            pltpu.VMEM((W, W), BF16),
            pltpu.VMEM((2, 5, 2, CAP, VIS), F32),
            pltpu.VMEM((2, CAP, TILE, VIS), F32),
            pltpu.VMEM((CAP * 64, 2 * VIS), BF16),
            dma((8,)),
            dma((8,)),
            dma((8,)),
            dma,
            dma,
            dma((8,)),
            dma((8,)),
            dma((8,)),
            dma((8,)),
            dma((8,)),
            dma((8,)),
            dma((16,)),
            dma((16,)),
            dma,
            dma,
        ],
        compiler_params=pltpu.CompilerParams(
            collective_id=0, has_side_effects=True, vmem_limit_bytes=55104 * 1024
        ),
    )(facet_strips, facet_offsets, column_offsets, row_offsets, tile_lists, tile_counts, uv_index)


def solution(mesh):
    in_specs = (
        P("facet", None, "col", None),
        P("facet", None),
        P("col"),
        P(),
        P("col", "facet", None),
        P("col", "facet"),
        P("col", "facet", None, None, None),
    )
    out_specs = P("col", "facet", None, None, None)
    return jax.shard_map(shards, mesh=mesh, in_specs=in_specs, out_specs=out_specs, check_vma=False)
```

```python
import math

import jax
import jax.numpy as jnp
from jax import lax
from jax.experimental import pallas as pl
from jax.experimental.pallas import tpu as pltpu
from jax.sharding import PartitionSpec as P

L = 8192
W = 128
S = 256
TILE = 32
NTOT = 65536
UV_STEPS = 4096
VIS = 1024
CAP = 8
FACETS = 64
LEN = 1024
MESH = pl.DeviceIdType.MESH
DEAL = 0
ORDER2 = ((0, 2), (0, 1), (0, 3), (1, 2), (0, 0), (1, 1), (1, 3), (1, 0))
AROUND = (4, -3, 3, -2, 2, -1, 1, 0)
FAR = ((1, 2), (1, 1), (1, 3), (0, 2), (1, 0), (0, 1), (0, 3))
F32 = jnp.float32
BF16 = jnp.bfloat16
I32 = jnp.int32


def unit(index):
    index = index & (NTOT - 1)
    index = jnp.where(index >= NTOT // 2, index - NTOT, index)
    angle = index.astype(F32) * (2.0 * math.pi / NTOT)
    return jnp.cos(angle), jnp.sin(angle)


def cmul(a, b):
    return a[0] * b[0] - a[1] * b[1], a[0] * b[1] + a[1] * b[0]


def iota(shape, dim):
    return lax.broadcasted_iota(I32, shape, dim)


def facet_of(x_hi, z, core):
    return (x_hi * 16 + z) * 2 + core


def group_facet(g, zg):
    return facet_of(g // 4, 2 * zg + g % 2, (g // 2) % 2)


def kernel(
    strip_ref,
    offsets_hbm,
    column_hbm,
    row_hbm,
    lists_hbm,
    counts_hbm,
    uv_ref,
    out_ref,
    offsets_ref,
    column_ref,
    row_ref,
    lists_ref,
    counts_ref,
    strip_v,
    uv_v,
    left_v,
    send1,
    recv1,
    block2,
    recv2,
    table_v,
    send3,
    recv3,
    recv4,
    small_v,
    recv_s,
    turn_v,
    ids_v,
    recv_i,
    pick_v,
    send5,
    recv5,
    pow_v,
    u_v,
    v_v,
    load_sem,
    s_s,
    r_s,
    s_i,
    r_i,
    s_1,
    r_1,
    s_2,
    r_2,
    s_3,
    r_3,
    s_4,
    r_4,
    s_5,
    r_5,
    word_2,
    word_3,
    word_4,
):
    facet = lax.axis_index("facet")
    col = lax.axis_index("col")
    x_hi = facet // 32
    z = (facet // 2) % 16
    core = facet % 2
    zg = z // 2
    zp = z % 2
    q_me = x_hi * 2 + core
    g_me = q_me * 2 + zp
    x_lo = col // 4
    y = col % 4

    def block_of(c, x):
        return (c // 4 + x + DEAL) % 2 * 4 + c % 4

    def col_of(block, x):
        return (block // 4 + x + DEAL) % 2 * 4 + block % 4

    target = block_of(col, x_hi)

    loads = [
        pltpu.make_async_copy(strip_ref.at[0, 0], strip_v.at[:, pl.ds(0, W)], load_sem.at[0]),
        pltpu.make_async_copy(strip_ref.at[0, 1], strip_v.at[:, pl.ds(W, W)], load_sem.at[1]),
        pltpu.make_async_copy(uv_ref.at[0, 0], uv_v, load_sem.at[2]),
        pltpu.make_async_copy(offsets_hbm, offsets_ref, load_sem.at[3]),
        pltpu.make_async_copy(row_hbm, row_ref, load_sem.at[4]),
        pltpu.make_async_copy(column_hbm, column_ref, load_sem.at[5]),
        pltpu.make_async_copy(lists_hbm, lists_ref, load_sem.at[6]),
        pltpu.make_async_copy(counts_hbm, counts_ref, load_sem.at[7]),
    ]
    for n in (3, 4, 0, 1, 5, 6, 7, 2):
        loads[n].start()

    barrier = pltpu.get_barrier_semaphore()

    def greet(f, c):
        pl.semaphore_signal(barrier, inc=1, device_id=(f, c), device_id_type=MESH)

    def along(i):
        return facet_of(x_hi, (z + i + 16) % 16, core)

    for i in (4, -4, 3, -3, 2, -2, 2 * zp - 1):
        greet(along(i), col)

    @pl.loop(1, 8)
    def _(i):
        greet(facet, (col + i) % 8)

    @pl.loop(1, 8)
    def _(i):
        greet(group_facet((g_me + i) % 8, zg), col)

    loads[3].wait()
    loads[4].wait()

    row0 = row_ref[0]
    cells = offsets_ref[0, 0] + col * LEN + iota((8, LEN), 1)
    base = unit((row0 + 8 * iota((8, LEN), 0)) * cells)
    scale = 1.0 / math.sqrt(L)
    step = unit(64 * cells)

    def left_body(t, value):
        nxt = cmul(value, step)
        at = pl.ds(pl.multiple_of(16 * t, 16), 16)
        left_v[at, :] = jnp.concatenate([value[0], nxt[0]], axis=0).astype(BF16)
        at = pl.ds(pl.multiple_of(S + 16 * t, 16), 16)
        left_v[at, :] = jnp.concatenate([value[1], nxt[1]], axis=0).astype(BF16)
        return cmul(nxt, step)

    lax.fori_loop(0, 16, left_body, (base[0] * scale, base[1] * scale))

    loads[0].wait()
    loads[1].wait()
    both = jnp.dot(left_v[...], strip_v[...], preferred_element_type=F32)
    real = both[:S, :W] + both[S:, W:]
    imag = both[:S, W:] - both[S:, :W]
    send1[...] = jnp.concatenate([real, imag], axis=1).astype(BF16).reshape(8, 32, 2 * W)

    pl.semaphore_wait(barrier, 21)

    def copy1(c):
        return pltpu.make_async_remote_copy(
            src_ref=send1.at[block_of(c, x_hi)], dst_ref=recv1.at[col], send_sem=s_1.at[c], recv_sem=r_1.at[col],
            device_id=(facet, c), device_id_type=MESH,
        )

    def from1(c):
        return pltpu.make_async_remote_copy(
            src_ref=send1.at[block_of(c, x_hi)], dst_ref=recv1.at[c], send_sem=s_1.at[c], recv_sem=r_1.at[c],
            device_id=(facet, c), device_id_type=MESH,
        )

    def col_at(far):
        return (x_lo + far[0]) % 2 * 4 + (y + far[1]) % 4

    for far in FAR:
        copy1(col_at(far)).start()

    def tell(sem, f):
        pl.semaphore_signal(sem, inc=1, device_id=(f, col), device_id_type=MESH)

    for g in range(8):

        @pl.when((block_of(col, g // 4) == g_me) & (g != g_me))
        def _():
            tell(word_2, group_facet(g, zg))

    tell(word_3, along(4))
    tell(word_3, along(-4))
    tell(word_4, facet_of(1 - x_hi, z, core))

    loads[6].wait()
    loads[7].wait()
    lanes = iota((8, W), 0)
    ids = jnp.full((8, W), -1, I32)
    for j in range(CAP):
        ids = jnp.where((lanes == j) & (j < counts_ref[0, 0]), lists_ref[0, 0, j], ids)
    ids_v[...] = ids
    small_v[...] = jnp.full((8, W), offsets_ref[0, 1], I32)
    recv_s[pl.ds(g_me, 1)] = small_v[...][None]

    def copy_s(g, dst):
        return pltpu.make_async_remote_copy(
            src_ref=small_v, dst_ref=recv_s.at[dst], send_sem=s_s.at[g], recv_sem=r_s.at[dst],
            device_id=(group_facet(g, zg), col), device_id_type=MESH,
        )

    copy_i = pltpu.make_async_remote_copy(
        src_ref=ids_v, dst_ref=recv_i, send_sem=s_i, recv_sem=r_i,
        device_id=(facet_of(x_hi, z, 1 - core), col), device_id_type=MESH,
    )
    copy_i.start()

    @pl.loop(1, 8)
    def _(i):
        copy_s((g_me + i) % 8, g_me).start()

    loads[5].wait()
    lane = iota((8, 2 * S), 1)
    sample = column_ref[0] + 256 * (32 * (lane // 64) + lane % 32)
    quarter = (NTOT // 4) * ((lane // 32) % 2)
    base_r = unit(iota((8, 2 * S), 0) * sample + quarter)
    step_r = unit(8 * sample)

    def right_body(t, value):
        nxt = cmul(value, step_r)
        re = jnp.concatenate([value[0], nxt[0]], axis=0)
        im = jnp.concatenate([value[1], nxt[1]], axis=0)
        top = pl.ds(pl.multiple_of(16 * t, 16), 16)
        low = pl.ds(pl.multiple_of(W + 16 * t, 16), 16)
        table_v[top, 0 : 2 * S] = re.astype(BF16)
        table_v[low, 0 : 2 * S] = im.astype(BF16)
        table_v[top, 2 * S :] = (-im).astype(BF16)
        table_v[low, 2 * S :] = re.astype(BF16)
        return cmul(nxt, step_r)

    lax.fori_loop(0, 8, right_body, base_r)

    total = send1[pl.ds(target, 1)].astype(F32)
    for far in FAR[::-1]:
        c = col_at(far)
        from1(c).wait_recv()
        total = total + recv1[pl.ds(c, 1)].astype(F32)
    block2[...] = total[0].astype(BF16)

    def copy2(c):
        return pltpu.make_async_remote_copy(
            src_ref=block2, dst_ref=recv2.at[g_me], send_sem=s_2.at[c], recv_sem=r_2.at[g_me],
            device_id=(group_facet(target, zg), c), device_id_type=MESH,
        )

    def from2(g):
        return pltpu.make_async_remote_copy(
            src_ref=block2, dst_ref=recv2.at[g], send_sem=s_2.at[g], recv_sem=r_2.at[g],
            device_id=(group_facet(g, zg), col_of(g_me, g // 4)), device_id_type=MESH,
        )

    @pl.when(target != g_me)
    def _():
        pl.semaphore_wait(word_2, 1)

    for x, dy in ORDER2:
        c = 4 * x + (y + dy) % 4

        @pl.when((target != g_me) | (c != col))
        def _():
            copy2(c).start()

    @pl.when(target == g_me)
    def _():
        recv2[pl.ds(g_me, 1)] = block2[...][None]

    loads[2].wait()
    for part in range(2):
        index = jnp.concatenate([uv_v[j, part : part + 1, :] for j in range(CAP)], axis=0)
        value = unit(index * (NTOT // UV_STEPS))
        for k in range(5):
            pow_v[part, k, 0] = value[0]
            pow_v[part, k, 1] = value[1]
            value = cmul(value, value)

    sub = iota((8, VIS), 0)

    def powers(part, j):
        def power(k):
            return tuple(
                jnp.broadcast_to(pow_v[part, k, h, pl.ds(j, 1), :], (8, VIS)) for h in range(2)
            )

        def chosen_power(k):
            re, im = power(k)
            on = (sub & (1 << k)) != 0
            return jnp.where(on, re, 1.0), jnp.where(on, im, 0.0)

        low = cmul(cmul(chosen_power(0), chosen_power(1)), chosen_power(2))
        sixteen = power(4)
        second = cmul(low, power(3))
        third = cmul(low, sixteen)
        fourth = cmul(second, sixteen)
        parts = (low, second, third, fourth)
        return tuple(jnp.concatenate([p[h] for p in parts], axis=0) for h in range(2))

    @pl.loop(0, CAP)
    def _(j):
        re, im = powers(0, j)
        u_v[0, j] = re * (1.0 / TILE)
        u_v[1, j] = im * (1.0 / TILE)
        re, im = powers(1, j)
        top = pl.ds(pl.multiple_of(64 * j, 32), 32)
        low = pl.ds(pl.multiple_of(64 * j + 32, 32), 32)
        v_v[top, 0:VIS] = re.astype(BF16)
        v_v[top, VIS:] = im.astype(BF16)
        v_v[low, 0:VIS] = (-im).astype(BF16)
        v_v[low, VIS:] = re.astype(BF16)

    @pl.loop(1, 8)
    def _(i):
        copy_s((g_me + i) % 8, (g_me + i) % 8).wait_recv()

    across = jnp.zeros((8, W), I32)
    for g in range(8):
        across = jnp.where(lanes == g, recv_s[g], across)
    across = jnp.concatenate([across] * 4, axis=1)
    turn = unit(across * sample)
    norm = 1.0 / math.sqrt(W * FACETS)
    turn_v[0] = turn[0] * norm
    turn_v[1] = turn[1] * norm

    copy_i.wait_recv()
    entry = iota((16, 4 * W), 1)
    diagonal = iota((16, 4 * W), 0) == entry % 16
    entry = entry // 16
    at_place = entry // 2 % 8
    entry = 32 * ((entry // 16 + x_hi) % 2) + 16 * core + 8 * (at_place % 2) + at_place // 2 + 4 * (entry % 2)
    for n, wanted_ref in enumerate((ids_v, recv_i)):
        for j in range(CAP):
            wanted = jnp.concatenate([wanted_ref[j : j + 1, :]] * 4, axis=1)
            pick = jnp.where((jnp.broadcast_to(wanted, entry.shape) == entry) & diagonal, 1.0, 0.0)
            at = 2 * 64 * (j // 4) + 64 * n + 16 * (j % 4)
            pick_v[at : at + 16, :] = pick.astype(BF16)

    @pl.loop(1, 8)
    def _(i):
        copy1((col + i) % 8).wait_send()
        copy_s((g_me + i) % 8, g_me).wait_send()

    copy_i.wait_send()

    terms = None
    for x in range(2):
        first = (x_hi + x) % 2 * 4

        @pl.loop(first, first + 4)
        def _(g):
            @pl.when((target != g_me) | (g != g_me))
            def _():
                from2(g).wait_recv()

        grid = jnp.dot(
            recv2[pl.ds(first, 4)].reshape(4 * 32, 2 * W), table_v[...], preferred_element_type=F32
        )
        for g in range(4):
            rows = grid[32 * g : 32 * g + 32]
            re, im = (turn_v[h, pl.ds(first + g, 1), :] for h in range(2))
            term = rows[:, : 2 * S] * re + rows[:, 2 * S :] * im
            terms = term if terms is None else terms + term

    low_half = iota((16, W), 1) < 64
    for v in range(4):
        top = terms[0:16, W * v : W * v + W]
        low = terms[16:32, W * v : W * v + W]
        send3[2 * v % 4, v // 2] = jnp.where(low_half, top, pltpu.roll(low, 64, 1)).astype(BF16)
        send3[(2 * v + 1) % 4, v // 2] = jnp.where(low_half, pltpu.roll(top, 64, 1), low).astype(BF16)

    def copy3(n, dst):
        return pltpu.make_async_remote_copy(
            src_ref=send3.at[n % 4], dst_ref=recv3.at[dst], send_sem=s_3.at[n], recv_sem=r_3.at[dst],
            device_id=(facet_of(x_hi, 2 * n + zp, core), col), device_id_type=MESH,
        )

    pl.semaphore_wait(word_3, 2)
    for i in (4, 3, 5, 2, 6, 1, 7):
        copy3((zg + i) % 8, zg).start()

    total = send3[pl.ds(zg % 4, 1)].astype(F32)
    for i in (1, 7, 2, 6, 3, 5, 4):
        n = (zg + i) % 8
        copy3(n, n).wait_recv()
        total = total + recv3[pl.ds(n, 1)].astype(F32)

    place = z % 8
    recv4[pl.ds(place, 1)] = total.astype(BF16)

    def copy4(x, i, dst):
        there = 8 * x + (place + i) % 8
        return pltpu.make_async_remote_copy(
            src_ref=recv4.at[place], dst_ref=recv4.at[dst], send_sem=s_4.at[there], recv_sem=r_4.at[dst],
            device_id=(facet_of((x_hi + x) % 2, (z + i) % 16, core), col), device_id_type=MESH,
        )

    pl.semaphore_wait(word_4, 1)
    for i in AROUND:
        copy4(1, i + 16, 8 + place).start()
    for i in AROUND[:-1]:
        copy4(0, i + 16, place).start()

    @pl.loop(0, 8)
    def _(c):
        @pl.when((target != g_me) | (c != col))
        def _():
            copy2(c).wait_send()

    @pl.loop(1, 8)
    def _(i):
        n = (place + i) % 8
        copy4(0, i, n).wait_recv()

    half = 2 * W
    near = jnp.dot(
        pick_v[:, :half], recv4[0:8].reshape(half, W), preferred_element_type=F32
    )

    @pl.loop(0, 8)
    def _(i):
        n = (place + i) % 8
        copy4(1, i, 8 + n).wait_recv()

    def copy5(h):
        return pltpu.make_async_remote_copy(
            src_ref=send5.at[h, 1], dst_ref=recv5.at[h], send_sem=s_5.at[h], recv_sem=r_5.at[h],
            device_id=(facet_of(x_hi, z, 1 - core), col), device_id_type=MESH,
        )

    for h in range(2):
        rows = slice(W * h, W * h + W)
        picks = near[rows] + jnp.dot(
            pick_v[rows, half:], recv4[8:16].reshape(half, W), preferred_element_type=F32
        )
        send5[h] = picks.astype(BF16).reshape(2, 64, W)
        copy5(h).start()

    @pl.loop(1, 8)
    def _(i):
        copy3((zg + i) % 8, zg).wait_send()
        copy4(0, i, place).wait_send()

    @pl.loop(0, 8)
    def _(i):
        copy4(1, i, 8 + place).wait_send()

    for h in range(2):
        copy5(h).wait_recv()
        chosen = send5[h, 0].astype(F32) + recv5[h].astype(F32)
        rows = []
        for i in range(4):
            tile = chosen[16 * i : 16 * i + 16]
            other = pltpu.roll(tile, 64, 1)
            if i % 2 == 0:
                top, low = jnp.where(low_half, tile, 0.0), jnp.where(low_half, other, 0.0)
            else:
                top, low = jnp.where(low_half, 0.0, other), jnp.where(low_half, 0.0, tile)
            here = jnp.concatenate([top, low], axis=0)
            none = jnp.zeros_like(here)
            rows.append(jnp.concatenate([here, none] if i < 2 else [none, here], axis=1))
        lhs = jnp.concatenate(rows, axis=0).astype(BF16)
        deep = slice(256 * h, 256 * h + 256)
        for k in range(0, VIS, 256):
            re = jnp.dot(lhs, v_v[deep, k : k + 256], preferred_element_type=F32)
            im = jnp.dot(lhs, v_v[deep, VIS + k : VIS + k + 256], preferred_element_type=F32)
            for i in range(4):
                j = 4 * h + i
                a = (re[32 * i : 32 * i + 32], im[32 * i : 32 * i + 32])
                b = (u_v[0, j, :, k : k + 256], u_v[1, j, :, k : k + 256])
                vis = cmul(a, b)
                for part in range(2):
                    out_ref[0, 0, j, part : part + 1, k : k + 256] = jnp.sum(
                        vis[part], axis=0, keepdims=True
                    )

    copy5(0).wait_send()
    copy5(1).wait_send()


def shards(
    facet_strips, facet_offsets, column_offsets, row_offsets, tile_lists, tile_counts, uv_index
):
    anywhere = pl.BlockSpec(memory_space=pl.ANY)
    dma = pltpu.SemaphoreType.DMA
    return pl.pallas_call(
        kernel,
        out_shape=jax.ShapeDtypeStruct((1, 1, CAP, 2, VIS), F32),
        in_specs=[anywhere] * 7,
        out_specs=pl.BlockSpec(memory_space=pltpu.VMEM),
        scratch_shapes=[
            pltpu.SMEM((1, 2), I32),
            pltpu.SMEM((1,), I32),
            pltpu.SMEM((1,), I32),
            pltpu.SMEM((1, 1, CAP), I32),
            pltpu.SMEM((1, 1), I32),
            pltpu.VMEM((LEN, 2 * W), BF16),
            pltpu.VMEM((CAP, 2, VIS), I32),
            pltpu.VMEM((2 * S, LEN), BF16),
            pltpu.VMEM((8, 32, 2 * W), BF16),
            pltpu.VMEM((8, 32, 2 * W), BF16),
            pltpu.VMEM((32, 2 * W), BF16),
            pltpu.VMEM((8, 32, 2 * W), BF16),
            pltpu.VMEM((2 * W, 4 * S), BF16),
            pltpu.VMEM((4, 2, 16, W), BF16),
            pltpu.VMEM((8, 2, 16, W), BF16),
            pltpu.VMEM((16, 2, 16, W), BF16),
            pltpu.VMEM((8, W), I32),
            pltpu.VMEM((8, 8, W), I32),
            pltpu.VMEM((2, 8, 2 * S), F32),
            pltpu.VMEM((8, W), I32),
            pltpu.VMEM((8, W), I32),
            pltpu.VMEM((2 * W, 4 * W), BF16),
            pltpu.VMEM((2, 2, 64, W), BF16),
            pltpu.VMEM((2, 64, W), BF16),
            pltpu.VMEM((2, 5, 2, CAP, VIS), F32),
            pltpu.VMEM((2, CAP, TILE, VIS), F32),
            pltpu.VMEM((CAP * 64, 2 * VIS), BF16),
            dma((8,)),
            dma((8,)),
            dma((8,)),
            dma,
            dma,
            dma((8,)),
            dma((8,)),
            dma((8,)),
            dma((8,)),
            dma((8,)),
            dma((8,)),
            dma((16,)),
            dma((16,)),
            dma((2,)),
            dma((2,)),
            pltpu.SemaphoreType.REGULAR,
            pltpu.SemaphoreType.REGULAR,
            pltpu.SemaphoreType.REGULAR,
        ],
        compiler_params=pltpu.CompilerParams(
            collective_id=0, has_side_effects=True, vmem_limit_bytes=55104 * 1024
        ),
    )(facet_strips, facet_offsets, column_offsets, row_offsets, tile_lists, tile_counts, uv_index)


def solution(mesh):
    in_specs = (
        P("facet", None, "col", None),
        P("facet", None),
        P("col"),
        P(),
        P("col", "facet", None),
        P("col", "facet"),
        P("col", "facet", None, None, None),
    )
    out_specs = P("col", "facet", None, None, None)
    return jax.shard_map(shards, mesh=mesh, in_specs=in_specs, out_specs=out_specs, check_vma=False)
```

```python
import math

import jax
import jax.numpy as jnp
from jax import lax
from jax.experimental import pallas as pl
from jax.experimental.pallas import tpu as pltpu
from jax.sharding import PartitionSpec as P

L = 8192
W = 128
S = 256
TILE = 32
NTOT = 65536
UV_STEPS = 4096
VIS = 1024
CAP = 8
FACETS = 64
LEN = 1024
MESH = pl.DeviceIdType.MESH
DEAL = 0
LINE = (4, -4, 3, -3, 2, -2)
ORDER2 = ((0, 2), (0, 1), (0, 3), (1, 2), (0, 0), (1, 1), (1, 3), (1, 0))
AROUND = (4, -3, 3, -2, 2, -1, 1, 0)
FAR = ((1, 2), (1, 1), (1, 3), (0, 2), (1, 0), (0, 1), (0, 3))
F32 = jnp.float32
BF16 = jnp.bfloat16
I32 = jnp.int32


def unit(index):
    index = index & (NTOT - 1)
    index = jnp.where(index >= NTOT // 2, index - NTOT, index)
    angle = index.astype(F32) * (2.0 * math.pi / NTOT)
    return jnp.cos(angle), jnp.sin(angle)


def cmul(a, b):
    return a[0] * b[0] - a[1] * b[1], a[0] * b[1] + a[1] * b[0]


def iota(shape, dim):
    return lax.broadcasted_iota(I32, shape, dim)


def facet_of(x_hi, z, core):
    return (x_hi * 16 + z) * 2 + core


def group_facet(g, zg):
    return facet_of(g // 4, 2 * zg + g % 2, (g // 2) % 2)


def kernel(
    strip_ref,
    offsets_hbm,
    column_hbm,
    row_hbm,
    lists_hbm,
    counts_hbm,
    uv_ref,
    out_ref,
    offsets_ref,
    column_ref,
    row_ref,
    lists_ref,
    counts_ref,
    strip_v,
    uv_v,
    left_v,
    send1,
    recv1,
    block2,
    recv2,
    table_v,
    send3,
    recv3,
    recv4,
    small_v,
    recv_s,
    turn_v,
    ids_v,
    recv_i,
    pick_v,
    send5,
    recv5,
    pow_v,
    u_v,
    v_v,
    load_sem,
    s_s,
    r_s,
    s_i,
    r_i,
    s_1,
    r_1,
    s_2,
    r_2,
    s_3,
    r_3,
    s_4,
    r_4,
    s_5,
    r_5,
    word_2,
    word_3,
    word_4,
    word_5,
):
    facet = lax.axis_index("facet")
    col = lax.axis_index("col")
    x_hi = facet // 32
    z = (facet // 2) % 16
    core = facet % 2
    zg = z // 2
    zp = z % 2
    q_me = x_hi * 2 + core
    g_me = q_me * 2 + zp
    x_lo = col // 4
    y = col % 4

    def block_of(c, x):
        return (c // 4 + x + DEAL) % 2 * 4 + c % 4

    def col_of(block, x):
        return (block // 4 + x + DEAL) % 2 * 4 + block % 4

    target = block_of(col, x_hi)

    loads = [
        pltpu.make_async_copy(strip_ref.at[0, 0], strip_v.at[:, pl.ds(0, W)], load_sem.at[0]),
        pltpu.make_async_copy(strip_ref.at[0, 1], strip_v.at[:, pl.ds(W, W)], load_sem.at[1]),
        pltpu.make_async_copy(uv_ref.at[0, 0], uv_v, load_sem.at[2]),
        pltpu.make_async_copy(offsets_hbm, offsets_ref, load_sem.at[3]),
        pltpu.make_async_copy(row_hbm, row_ref, load_sem.at[4]),
        pltpu.make_async_copy(column_hbm, column_ref, load_sem.at[5]),
        pltpu.make_async_copy(lists_hbm, lists_ref, load_sem.at[6]),
        pltpu.make_async_copy(counts_hbm, counts_ref, load_sem.at[7]),
    ]
    for n in (3, 4, 0, 1, 5, 6, 7, 2):
        loads[n].start()

    barrier = pltpu.get_barrier_semaphore()

    def greet(f, c):
        pl.semaphore_signal(barrier, inc=1, device_id=(f, c), device_id_type=MESH)

    def along(i):
        return facet_of(x_hi, (z + i + 16) % 16, core)

    def rank(p):
        return p + 4 * (p // 8 - p // 12) + p // 12 * (23 - 2 * p)

    def is_later(i):
        return (rank((z + i + 16) % 16) - rank(z) + 15) // 16

    @pl.loop(1, 8)
    def _(i):
        greet(facet, (col + i) % 8)

    @pl.loop(1, 8)
    def _(i):
        greet(group_facet((g_me + i) % 8, zg), col)

    later = 0
    for i in LINE + (2 * zp - 1,):
        later = later + is_later(i)

        @pl.when(is_later(i) == 1)
        def _():
            greet(along(i), col)

    loads[3].wait()
    loads[4].wait()

    row0 = row_ref[0]
    cells = offsets_ref[0, 0] + col * LEN + iota((8, LEN), 1)
    base = unit((row0 + 8 * iota((8, LEN), 0)) * cells)
    scale = 1.0 / math.sqrt(L)
    step = unit(64 * cells)

    def left_body(t, value):
        nxt = cmul(value, step)
        at = pl.ds(pl.multiple_of(16 * t, 16), 16)
        left_v[at, :] = jnp.concatenate([value[0], nxt[0]], axis=0).astype(BF16)
        at = pl.ds(pl.multiple_of(S + 16 * t, 16), 16)
        left_v[at, :] = jnp.concatenate([value[1], nxt[1]], axis=0).astype(BF16)
        return cmul(nxt, step)

    lax.fori_loop(0, 16, left_body, (base[0] * scale, base[1] * scale))

    loads[0].wait()
    loads[1].wait()
    both = jnp.dot(left_v[...], strip_v[...], preferred_element_type=F32)
    real = both[:S, :W] + both[S:, W:]
    imag = both[:S, W:] - both[S:, :W]
    send1[...] = jnp.concatenate([real, imag], axis=1).astype(BF16).reshape(8, 32, 2 * W)

    pl.semaphore_wait(barrier, 21 - later)

    def copy1(c):
        return pltpu.make_async_remote_copy(
            src_ref=send1.at[block_of(c, x_hi)], dst_ref=recv1.at[col], send_sem=s_1.at[c], recv_sem=r_1.at[col],
            device_id=(facet, c), device_id_type=MESH,
        )

    def from1(c):
        return pltpu.make_async_remote_copy(
            src_ref=send1.at[block_of(c, x_hi)], dst_ref=recv1.at[c], send_sem=s_1.at[c], recv_sem=r_1.at[c],
            device_id=(facet, c), device_id_type=MESH,
        )

    def col_at(far):
        return (x_lo + far[0]) % 2 * 4 + (y + far[1]) % 4

    for far in FAR:
        copy1(col_at(far)).start()

    def tell(sem, f):
        pl.semaphore_signal(sem, inc=1, device_id=(f, col), device_id_type=MESH)

    for g in range(8):

        @pl.when((block_of(col, g // 4) == g_me) & (g != g_me))
        def _():
            tell(word_2, group_facet(g, zg))

    for i in LINE + (2 * zp - 1,):

        @pl.when(is_later(i) == 0)
        def _():
            tell(word_3, along(i))

    loads[6].wait()
    loads[7].wait()
    lanes = iota((8, W), 0)
    ids = jnp.full((8, W), -1, I32)
    for j in range(CAP):
        ids = jnp.where((lanes == j) & (j < counts_ref[0, 0]), lists_ref[0, 0, j], ids)
    ids_v[...] = ids
    small_v[...] = jnp.full((8, W), offsets_ref[0, 1], I32)
    recv_s[pl.ds(g_me, 1)] = small_v[...][None]

    def copy_s(g, dst):
        return pltpu.make_async_remote_copy(
            src_ref=small_v, dst_ref=recv_s.at[dst], send_sem=s_s.at[g], recv_sem=r_s.at[dst],
            device_id=(group_facet(g, zg), col), device_id_type=MESH,
        )

    copy_i = pltpu.make_async_remote_copy(
        src_ref=ids_v, dst_ref=recv_i, send_sem=s_i, recv_sem=r_i,
        device_id=(facet_of(x_hi, z, 1 - core), col), device_id_type=MESH,
    )
    copy_i.start()

    @pl.loop(1, 8)
    def _(i):
        copy_s((g_me + i) % 8, g_me).start()

    loads[5].wait()
    lane = iota((8, 2 * S), 1)
    sample = column_ref[0] + 256 * (32 * (lane // 64) + lane % 32)
    quarter = (NTOT // 4) * ((lane // 32) % 2)
    base_r = unit(iota((8, 2 * S), 0) * sample + quarter)
    step_r = unit(8 * sample)

    def right_body(t, value):
        nxt = cmul(value, step_r)
        re = jnp.concatenate([value[0], nxt[0]], axis=0)
        im = jnp.concatenate([value[1], nxt[1]], axis=0)
        top = pl.ds(pl.multiple_of(16 * t, 16), 16)
        low = pl.ds(pl.multiple_of(W + 16 * t, 16), 16)
        table_v[top, 0 : 2 * S] = re.astype(BF16)
        table_v[low, 0 : 2 * S] = im.astype(BF16)
        table_v[top, 2 * S :] = (-im).astype(BF16)
        table_v[low, 2 * S :] = re.astype(BF16)
        return cmul(nxt, step_r)

    lax.fori_loop(0, 8, right_body, base_r)

    total = send1[pl.ds(target, 1)].astype(F32)
    for far in FAR[::-1]:
        c = col_at(far)
        from1(c).wait_recv()
        total = total + recv1[pl.ds(c, 1)].astype(F32)
    block2[...] = total[0].astype(BF16)

    def copy2(c):
        return pltpu.make_async_remote_copy(
            src_ref=block2, dst_ref=recv2.at[g_me], send_sem=s_2.at[c], recv_sem=r_2.at[g_me],
            device_id=(group_facet(target, zg), c), device_id_type=MESH,
        )

    def from2(g):
        return pltpu.make_async_remote_copy(
            src_ref=block2, dst_ref=recv2.at[g], send_sem=s_2.at[g], recv_sem=r_2.at[g],
            device_id=(group_facet(g, zg), col_of(g_me, g // 4)), device_id_type=MESH,
        )

    @pl.when(target != g_me)
    def _():
        pl.semaphore_wait(word_2, 1)

    for x, dy in ORDER2:
        c = 4 * x + (y + dy) % 4

        @pl.when((target != g_me) | (c != col))
        def _():
            copy2(c).start()

    @pl.when(target == g_me)
    def _():
        recv2[pl.ds(g_me, 1)] = block2[...][None]

    @pl.when(later > 0)
    def _():
        pl.semaphore_wait(word_3, later)

    tell(word_5, along(4))
    tell(word_5, along(-4))
    tell(word_4, facet_of(1 - x_hi, z, core))

    loads[2].wait()
    for part in range(2):
        index = jnp.concatenate([uv_v[j, part : part + 1, :] for j in range(CAP)], axis=0)
        value = unit(index * (NTOT // UV_STEPS))
        for k in range(5):
            pow_v[part, k, 0] = value[0]
            pow_v[part, k, 1] = value[1]
            value = cmul(value, value)

    sub = iota((8, VIS), 0)

    def powers(part, j):
        def power(k):
            return tuple(
                jnp.broadcast_to(pow_v[part, k, h, pl.ds(j, 1), :], (8, VIS)) for h in range(2)
            )

        def chosen_power(k):
            re, im = power(k)
            on = (sub & (1 << k)) != 0
            return jnp.where(on, re, 1.0), jnp.where(on, im, 0.0)

        low = cmul(cmul(chosen_power(0), chosen_power(1)), chosen_power(2))
        sixteen = power(4)
        second = cmul(low, power(3))
        third = cmul(low, sixteen)
        fourth = cmul(second, sixteen)
        parts = (low, second, third, fourth)
        return tuple(jnp.concatenate([p[h] for p in parts], axis=0) for h in range(2))

    @pl.loop(0, CAP)
    def _(j):
        re, im = powers(0, j)
        u_v[0, j] = re * (1.0 / TILE)
        u_v[1, j] = im * (1.0 / TILE)
        re, im = powers(1, j)
        top = pl.ds(pl.multiple_of(64 * j, 32), 32)
        low = pl.ds(pl.multiple_of(64 * j + 32, 32), 32)
        v_v[top, 0:VIS] = re.astype(BF16)
        v_v[top, VIS:] = im.astype(BF16)
        v_v[low, 0:VIS] = (-im).astype(BF16)
        v_v[low, VIS:] = re.astype(BF16)

    @pl.loop(1, 8)
    def _(i):
        copy_s((g_me + i) % 8, (g_me + i) % 8).wait_recv()

    across = jnp.zeros((8, W), I32)
    for g in range(8):
        across = jnp.where(lanes == g, recv_s[g], across)
    across = jnp.concatenate([across] * 4, axis=1)
    turn = unit(across * sample)
    norm = 1.0 / math.sqrt(W * FACETS)
    turn_v[0] = turn[0] * norm
    turn_v[1] = turn[1] * norm

    copy_i.wait_recv()
    entry = iota((16, 4 * W), 1)
    diagonal = iota((16, 4 * W), 0) == entry % 16
    entry = entry // 16
    at_place = entry // 2 % 8
    entry = 32 * ((entry // 16 + x_hi) % 2) + 16 * core + 8 * (at_place % 2) + at_place // 2 + 4 * (entry % 2)
    for n, wanted_ref in enumerate((ids_v, recv_i)):
        for j in range(CAP):
            wanted = jnp.concatenate([wanted_ref[j : j + 1, :]] * 4, axis=1)
            pick = jnp.where((jnp.broadcast_to(wanted, entry.shape) == entry) & diagonal, 1.0, 0.0)
            at = 2 * 64 * (j // 4) + 64 * n + 16 * (j % 4)
            pick_v[at : at + 16, :] = pick.astype(BF16)

    @pl.loop(1, 8)
    def _(i):
        copy1((col + i) % 8).wait_send()
        copy_s((g_me + i) % 8, g_me).wait_send()

    copy_i.wait_send()

    terms = None
    for x in range(2):
        first = (x_hi + x) % 2 * 4

        @pl.loop(first, first + 4)
        def _(g):
            @pl.when((target != g_me) | (g != g_me))
            def _():
                from2(g).wait_recv()

        grid = jnp.dot(
            recv2[pl.ds(first, 4)].reshape(4 * 32, 2 * W), table_v[...], preferred_element_type=F32
        )
        for g in range(4):
            rows = grid[32 * g : 32 * g + 32]
            re, im = (turn_v[h, pl.ds(first + g, 1), :] for h in range(2))
            term = rows[:, : 2 * S] * re + rows[:, 2 * S :] * im
            terms = term if terms is None else terms + term

    low_half = iota((16, W), 1) < 64
    for v in range(4):
        top = terms[0:16, W * v : W * v + W]
        low = terms[16:32, W * v : W * v + W]
        send3[2 * v % 4, v // 2] = jnp.where(low_half, top, pltpu.roll(low, 64, 1)).astype(BF16)
        send3[(2 * v + 1) % 4, v // 2] = jnp.where(low_half, pltpu.roll(top, 64, 1), low).astype(BF16)

    def copy3(n, dst):
        return pltpu.make_async_remote_copy(
            src_ref=send3.at[n % 4], dst_ref=recv3.at[dst], send_sem=s_3.at[n], recv_sem=r_3.at[dst],
            device_id=(facet_of(x_hi, 2 * n + zp, core), col), device_id_type=MESH,
        )

    pl.semaphore_wait(word_5, 2)
    for i in (4, 3, 5, 2, 6, 1, 7):
        copy3((zg + i) % 8, zg).start()

    total = send3[pl.ds(zg % 4, 1)].astype(F32)
    for i in (1, 7, 2, 6, 3, 5, 4):
        n = (zg + i) % 8
        copy3(n, n).wait_recv()
        total = total + recv3[pl.ds(n, 1)].astype(F32)

    place = z % 8
    recv4[pl.ds(place, 1)] = total.astype(BF16)

    def copy4(x, i, dst):
        there = 8 * x + (place + i) % 8
        return pltpu.make_async_remote_copy(
            src_ref=recv4.at[place], dst_ref=recv4.at[dst], send_sem=s_4.at[there], recv_sem=r_4.at[dst],
            device_id=(facet_of((x_hi + x) % 2, (z + i) % 16, core), col), device_id_type=MESH,
        )

    pl.semaphore_wait(word_4, 1)
    for i in AROUND:
        copy4(1, i + 16, 8 + place).start()
    for i in AROUND[:-1]:
        copy4(0, i + 16, place).start()

    @pl.loop(0, 8)
    def _(c):
        @pl.when((target != g_me) | (c != col))
        def _():
            copy2(c).wait_send()

    @pl.loop(1, 8)
    def _(i):
        n = (place + i) % 8
        copy4(0, i, n).wait_recv()

    half = 2 * W
    near = jnp.dot(
        pick_v[:, :half], recv4[0:8].reshape(half, W), preferred_element_type=F32
    )

    @pl.loop(0, 8)
    def _(i):
        n = (place + i) % 8
        copy4(1, i, 8 + n).wait_recv()

    def copy5(h):
        return pltpu.make_async_remote_copy(
            src_ref=send5.at[h, 1], dst_ref=recv5.at[h], send_sem=s_5.at[h], recv_sem=r_5.at[h],
            device_id=(facet_of(x_hi, z, 1 - core), col), device_id_type=MESH,
        )

    for h in range(2):
        rows = slice(W * h, W * h + W)
        picks = near[rows] + jnp.dot(
            pick_v[rows, half:], recv4[8:16].reshape(half, W), preferred_element_type=F32
        )
        send5[h] = picks.astype(BF16).reshape(2, 64, W)
        copy5(h).start()

    @pl.loop(1, 8)
    def _(i):
        copy3((zg + i) % 8, zg).wait_send()
        copy4(0, i, place).wait_send()

    @pl.loop(0, 8)
    def _(i):
        copy4(1, i, 8 + place).wait_send()

    for h in range(2):
        copy5(h).wait_recv()
        chosen = send5[h, 0].astype(F32) + recv5[h].astype(F32)
        rows = []
        for i in range(4):
            tile = chosen[16 * i : 16 * i + 16]
            other = pltpu.roll(tile, 64, 1)
            if i % 2 == 0:
                top, low = jnp.where(low_half, tile, 0.0), jnp.where(low_half, other, 0.0)
            else:
                top, low = jnp.where(low_half, 0.0, other), jnp.where(low_half, 0.0, tile)
            here = jnp.concatenate([top, low], axis=0)
            none = jnp.zeros_like(here)
            rows.append(jnp.concatenate([here, none] if i < 2 else [none, here], axis=1))
        lhs = jnp.concatenate(rows, axis=0).astype(BF16)
        deep = slice(256 * h, 256 * h + 256)
        for k in range(0, VIS, 256):
            re = jnp.dot(lhs, v_v[deep, k : k + 256], preferred_element_type=F32)
            im = jnp.dot(lhs, v_v[deep, VIS + k : VIS + k + 256], preferred_element_type=F32)
            for i in range(4):
                j = 4 * h + i
                a = (re[32 * i : 32 * i + 32], im[32 * i : 32 * i + 32])
                b = (u_v[0, j, :, k : k + 256], u_v[1, j, :, k : k + 256])
                vis = cmul(a, b)
                for part in range(2):
                    out_ref[0, 0, j, part : part + 1, k : k + 256] = jnp.sum(
                        vis[part], axis=0, keepdims=True
                    )

    copy5(0).wait_send()
    copy5(1).wait_send()


def shards(
    facet_strips, facet_offsets, column_offsets, row_offsets, tile_lists, tile_counts, uv_index
):
    anywhere = pl.BlockSpec(memory_space=pl.ANY)
    dma = pltpu.SemaphoreType.DMA
    return pl.pallas_call(
        kernel,
        out_shape=jax.ShapeDtypeStruct((1, 1, CAP, 2, VIS), F32),
        in_specs=[anywhere] * 7,
        out_specs=pl.BlockSpec(memory_space=pltpu.VMEM),
        scratch_shapes=[
            pltpu.SMEM((1, 2), I32),
            pltpu.SMEM((1,), I32),
            pltpu.SMEM((1,), I32),
            pltpu.SMEM((1, 1, CAP), I32),
            pltpu.SMEM((1, 1), I32),
            pltpu.VMEM((LEN, 2 * W), BF16),
            pltpu.VMEM((CAP, 2, VIS), I32),
            pltpu.VMEM((2 * S, LEN), BF16),
            pltpu.VMEM((8, 32, 2 * W), BF16),
            pltpu.VMEM((8, 32, 2 * W), BF16),
            pltpu.VMEM((32, 2 * W), BF16),
            pltpu.VMEM((8, 32, 2 * W), BF16),
            pltpu.VMEM((2 * W, 4 * S), BF16),
            pltpu.VMEM((4, 2, 16, W), BF16),
            pltpu.VMEM((8, 2, 16, W), BF16),
            pltpu.VMEM((16, 2, 16, W), BF16),
            pltpu.VMEM((8, W), I32),
            pltpu.VMEM((8, 8, W), I32),
            pltpu.VMEM((2, 8, 2 * S), F32),
            pltpu.VMEM((8, W), I32),
            pltpu.VMEM((8, W), I32),
            pltpu.VMEM((2 * W, 4 * W), BF16),
            pltpu.VMEM((2, 2, 64, W), BF16),
            pltpu.VMEM((2, 64, W), BF16),
            pltpu.VMEM((2, 5, 2, CAP, VIS), F32),
            pltpu.VMEM((2, CAP, TILE, VIS), F32),
            pltpu.VMEM((CAP * 64, 2 * VIS), BF16),
            dma((8,)),
            dma((8,)),
            dma((8,)),
            dma,
            dma,
            dma((8,)),
            dma((8,)),
            dma((8,)),
            dma((8,)),
            dma((8,)),
            dma((8,)),
            dma((16,)),
            dma((16,)),
            dma((2,)),
            dma((2,)),
            pltpu.SemaphoreType.REGULAR,
            pltpu.SemaphoreType.REGULAR,
            pltpu.SemaphoreType.REGULAR,
            pltpu.SemaphoreType.REGULAR,
        ],
        compiler_params=pltpu.CompilerParams(
            collective_id=0, has_side_effects=True, vmem_limit_bytes=55104 * 1024
        ),
    )(facet_strips, facet_offsets, column_offsets, row_offsets, tile_lists, tile_counts, uv_index)


def solution(mesh):
    in_specs = (
        P("facet", None, "col", None),
        P("facet", None),
        P("col"),
        P(),
        P("col", "facet", None),
        P("col", "facet"),
        P("col", "facet", None, None, None),
    )
    out_specs = P("col", "facet", None, None, None)
    return jax.shard_map(shards, mesh=mesh, in_specs=in_specs, out_specs=out_specs, check_vma=False)
```

```python
import math

import jax
import jax.numpy as jnp
from jax import lax
from jax.experimental import pallas as pl
from jax.experimental.pallas import tpu as pltpu
from jax.sharding import PartitionSpec as P

L = 8192
W = 128
S = 256
TILE = 32
NTOT = 65536
UV_STEPS = 4096
VIS = 1024
CAP = 8
FACETS = 64
LEN = 1024
MESH = pl.DeviceIdType.MESH
DEAL = 0
LINE = (4, -4, 3, -3, 2, -2)
ORDER2 = ((1, 2), (1, 1), (1, 3), (0, 2), (1, 0), (0, 1), (0, 3), (0, 0))
FAR = ((1, 2), (1, 1), (1, 3), (0, 2), (1, 0), (0, 1), (0, 3))
F32 = jnp.float32
BF16 = jnp.bfloat16
I32 = jnp.int32


def unit(index):
    index = index & (NTOT - 1)
    index = jnp.where(index >= NTOT // 2, index - NTOT, index)
    angle = index.astype(F32) * (2.0 * math.pi / NTOT)
    return jnp.cos(angle), jnp.sin(angle)


def cmul(a, b):
    return a[0] * b[0] - a[1] * b[1], a[0] * b[1] + a[1] * b[0]


def iota(shape, dim):
    return lax.broadcasted_iota(I32, shape, dim)


def facet_of(x_hi, z, core):
    return (x_hi * 16 + z) * 2 + core


def group_facet(g, zg):
    return facet_of(g // 4, 2 * zg + g % 2, (g // 2) % 2)


def kernel(
    strip_ref,
    offsets_hbm,
    column_hbm,
    row_hbm,
    lists_hbm,
    counts_hbm,
    uv_ref,
    out_ref,
    offsets_ref,
    column_ref,
    row_ref,
    lists_ref,
    counts_ref,
    strip_v,
    uv_v,
    left_v,
    send1,
    recv1,
    block2,
    recv2,
    table_v,
    send3,
    recv3,
    recv4,
    small_v,
    recv_s,
    turn_v,
    ids_v,
    recv_i,
    pick_v,
    send5,
    recv5,
    pow_v,
    u_v,
    v_v,
    load_sem,
    s_s,
    r_s,
    s_i,
    r_i,
    s_1,
    r_1,
    s_2,
    r_2,
    s_3,
    r_3,
    s_4,
    r_4,
    s_5,
    r_5,
    word_2,
    word_3,
    word_4,
    word_5,
):
    facet = lax.axis_index("facet")
    col = lax.axis_index("col")
    x_hi = facet // 32
    z = (facet // 2) % 16
    core = facet % 2
    zg = z // 2
    zp = z % 2
    q_me = x_hi * 2 + core
    g_me = q_me * 2 + zp
    x_lo = col // 4
    y = col % 4

    def block_of(c, x):
        return (c // 4 + x + DEAL) % 2 * 4 + c % 4

    def col_of(block, x):
        return (block // 4 + x + DEAL) % 2 * 4 + block % 4

    target = block_of(col, x_hi)

    loads = [
        pltpu.make_async_copy(strip_ref.at[0, 0], strip_v.at[:, pl.ds(0, W)], load_sem.at[0]),
        pltpu.make_async_copy(strip_ref.at[0, 1], strip_v.at[:, pl.ds(W, W)], load_sem.at[1]),
        pltpu.make_async_copy(uv_ref.at[0, 0], uv_v, load_sem.at[2]),
        pltpu.make_async_copy(offsets_hbm, offsets_ref, load_sem.at[3]),
        pltpu.make_async_copy(row_hbm, row_ref, load_sem.at[4]),
        pltpu.make_async_copy(column_hbm, column_ref, load_sem.at[5]),
        pltpu.make_async_copy(lists_hbm, lists_ref, load_sem.at[6]),
        pltpu.make_async_copy(counts_hbm, counts_ref, load_sem.at[7]),
    ]
    for n in (3, 4, 0, 1, 5, 6, 7, 2):
        loads[n].start()

    barrier = pltpu.get_barrier_semaphore()

    def greet(f, c):
        pl.semaphore_signal(barrier, inc=1, device_id=(f, c), device_id_type=MESH)

    def along(i):
        return facet_of(x_hi, (z + i + 16) % 16, core)

    def rank(p):
        return p + 4 * (p // 8 - p // 12) + p // 12 * (23 - 2 * p)

    def is_later(i):
        return (rank((z + i + 16) % 16) - rank(z) + 15) // 16

    @pl.loop(1, 8)
    def _(i):
        greet(facet, (col + i) % 8)

    @pl.loop(1, 8)
    def _(i):
        greet(group_facet((g_me + i) % 8, zg), col)

    later = 0
    for i in LINE + (2 * zp - 1,):
        later = later + is_later(i)

        @pl.when(is_later(i) == 1)
        def _():
            greet(along(i), col)

    loads[3].wait()
    loads[4].wait()

    row0 = row_ref[0]
    cells = offsets_ref[0, 0] + col * LEN + iota((8, LEN), 1)
    base = unit((row0 + 8 * iota((8, LEN), 0)) * cells)
    scale = 1.0 / math.sqrt(L)
    step = unit(64 * cells)

    def left_body(t, value):
        nxt = cmul(value, step)
        at = pl.ds(pl.multiple_of(16 * t, 16), 16)
        left_v[at, :] = jnp.concatenate([value[0], nxt[0]], axis=0).astype(BF16)
        at = pl.ds(pl.multiple_of(S + 16 * t, 16), 16)
        left_v[at, :] = jnp.concatenate([value[1], nxt[1]], axis=0).astype(BF16)
        return cmul(nxt, step)

    lax.fori_loop(0, 16, left_body, (base[0] * scale, base[1] * scale))

    loads[0].wait()
    loads[1].wait()
    both = jnp.dot(left_v[...], strip_v[...], preferred_element_type=F32)
    real = both[:S, :W] + both[S:, W:]
    imag = both[:S, W:] - both[S:, :W]
    send1[...] = jnp.concatenate([real, imag], axis=1).astype(BF16).reshape(8, 32, 2 * W)

    pl.semaphore_wait(barrier, 21 - later)

    def copy1(c):
        return pltpu.make_async_remote_copy(
            src_ref=send1.at[block_of(c, x_hi)], dst_ref=recv1.at[col], send_sem=s_1.at[c], recv_sem=r_1.at[col],
            device_id=(facet, c), device_id_type=MESH,
        )

    def from1(c):
        return pltpu.make_async_remote_copy(
            src_ref=send1.at[block_of(c, x_hi)], dst_ref=recv1.at[c], send_sem=s_1.at[c], recv_sem=r_1.at[c],
            device_id=(facet, c), device_id_type=MESH,
        )

    def col_at(far):
        return (x_lo + far[0]) % 2 * 4 + (y + far[1]) % 4

    for far in FAR:
        copy1(col_at(far)).start()

    def tell(sem, f):
        pl.semaphore_signal(sem, inc=1, device_id=(f, col), device_id_type=MESH)

    for g in range(8):

        @pl.when((block_of(col, g // 4) == g_me) & (g != g_me))
        def _():
            tell(word_2, group_facet(g, zg))

    for i in LINE + (2 * zp - 1,):

        @pl.when(is_later(i) == 0)
        def _():
            tell(word_3, along(i))

    loads[6].wait()
    loads[7].wait()
    lanes = iota((8, W), 0)
    ids = jnp.full((8, W), -1, I32)
    for j in range(CAP):
        ids = jnp.where((lanes == j) & (j < counts_ref[0, 0]), lists_ref[0, 0, j], ids)
    ids_v[...] = ids
    small_v[...] = jnp.full((8, W), offsets_ref[0, 1], I32)
    recv_s[pl.ds(g_me, 1)] = small_v[...][None]

    def copy_s(g, dst):
        return pltpu.make_async_remote_copy(
            src_ref=small_v, dst_ref=recv_s.at[dst], send_sem=s_s.at[g], recv_sem=r_s.at[dst],
            device_id=(group_facet(g, zg), col), device_id_type=MESH,
        )

    copy_i = pltpu.make_async_remote_copy(
        src_ref=ids_v, dst_ref=recv_i, send_sem=s_i, recv_sem=r_i,
        device_id=(facet_of(x_hi, z, 1 - core), col), device_id_type=MESH,
    )
    copy_i.start()

    @pl.loop(1, 8)
    def _(i):
        copy_s((g_me + i) % 8, g_me).start()

    loads[5].wait()
    lane = iota((8, 2 * S), 1)
    sample = column_ref[0] + 256 * (32 * (lane // 64) + lane % 32)
    quarter = (NTOT // 4) * ((lane // 32) % 2)
    base_r = unit(iota((8, 2 * S), 0) * sample + quarter)
    step_r = unit(8 * sample)

    def right_body(t, value):
        nxt = cmul(value, step_r)
        re = jnp.concatenate([value[0], nxt[0]], axis=0)
        im = jnp.concatenate([value[1], nxt[1]], axis=0)
        top = pl.ds(pl.multiple_of(16 * t, 16), 16)
        low = pl.ds(pl.multiple_of(W + 16 * t, 16), 16)
        table_v[top, 0 : 2 * S] = re.astype(BF16)
        table_v[low, 0 : 2 * S] = im.astype(BF16)
        table_v[top, 2 * S :] = (-im).astype(BF16)
        table_v[low, 2 * S :] = re.astype(BF16)
        return cmul(nxt, step_r)

    lax.fori_loop(0, 8, right_body, base_r)

    total = send1[pl.ds(target, 1)].astype(F32)
    for far in FAR[::-1]:
        c = col_at(far)
        from1(c).wait_recv()
        total = total + recv1[pl.ds(c, 1)].astype(F32)
    block2[...] = total[0].astype(BF16)

    def copy2(c):
        return pltpu.make_async_remote_copy(
            src_ref=block2, dst_ref=recv2.at[g_me], send_sem=s_2.at[c], recv_sem=r_2.at[g_me],
            device_id=(group_facet(target, zg), c), device_id_type=MESH,
        )

    def from2(g):
        return pltpu.make_async_remote_copy(
            src_ref=block2, dst_ref=recv2.at[g], send_sem=s_2.at[g], recv_sem=r_2.at[g],
            device_id=(group_facet(g, zg), col_of(g_me, g // 4)), device_id_type=MESH,
        )

    @pl.when(target != g_me)
    def _():
        pl.semaphore_wait(word_2, 1)

    for x, dy in ORDER2:
        c = 4 * x + (y + dy) % 4

        @pl.when((target != g_me) | (c != col))
        def _():
            copy2(c).start()

    @pl.when(target == g_me)
    def _():
        recv2[pl.ds(g_me, 1)] = block2[...][None]

    @pl.when(later > 0)
    def _():
        pl.semaphore_wait(word_3, later)

    tell(word_5, along(4))
    tell(word_5, along(-4))
    tell(word_4, facet_of(1 - x_hi, z, core))

    loads[2].wait()
    for part in range(2):
        index = jnp.concatenate([uv_v[j, part : part + 1, :] for j in range(CAP)], axis=0)
        value = unit(index * (NTOT // UV_STEPS))
        for k in range(5):
            pow_v[part, k, 0] = value[0]
            pow_v[part, k, 1] = value[1]
            value = cmul(value, value)

    sub = iota((8, VIS), 0)

    def powers(part, j):
        def power(k):
            return tuple(
                jnp.broadcast_to(pow_v[part, k, h, pl.ds(j, 1), :], (8, VIS)) for h in range(2)
            )

        def chosen_power(k):
            re, im = power(k)
            on = (sub & (1 << k)) != 0
            return jnp.where(on, re, 1.0), jnp.where(on, im, 0.0)

        low = cmul(cmul(chosen_power(0), chosen_power(1)), chosen_power(2))
        sixteen = power(4)
        second = cmul(low, power(3))
        third = cmul(low, sixteen)
        fourth = cmul(second, sixteen)
        parts = (low, second, third, fourth)
        return tuple(jnp.concatenate([p[h] for p in parts], axis=0) for h in range(2))

    @pl.loop(0, CAP)
    def _(j):
        re, im = powers(0, j)
        u_v[0, j] = re * (1.0 / TILE)
        u_v[1, j] = im * (1.0 / TILE)
        re, im = powers(1, j)
        top = pl.ds(pl.multiple_of(64 * j, 32), 32)
        low = pl.ds(pl.multiple_of(64 * j + 32, 32), 32)
        v_v[top, 0:VIS] = re.astype(BF16)
        v_v[top, VIS:] = im.astype(BF16)
        v_v[low, 0:VIS] = (-im).astype(BF16)
        v_v[low, VIS:] = re.astype(BF16)

    @pl.loop(1, 8)
    def _(i):
        copy_s((g_me + i) % 8, (g_me + i) % 8).wait_recv()

    across = jnp.zeros((8, W), I32)
    for g in range(8):
        across = jnp.where(lanes == g, recv_s[g], across)
    across = jnp.concatenate([across] * 4, axis=1)
    turn = unit(across * sample)
    norm = 1.0 / math.sqrt(W * FACETS)
    turn_v[0] = turn[0] * norm
    turn_v[1] = turn[1] * norm

    copy_i.wait_recv()
    entry = iota((16, 4 * W), 1)
    diagonal = iota((16, 4 * W), 0) == entry % 16
    entry = entry // 16
    at_place = entry // 2 % 8
    entry = 32 * ((entry // 16 + x_hi) % 2) + 16 * core + 8 * (at_place % 2) + at_place // 2 + 4 * (entry % 2)
    for n, wanted_ref in enumerate((ids_v, recv_i)):
        for j in range(CAP):
            wanted = jnp.concatenate([wanted_ref[j : j + 1, :]] * 4, axis=1)
            pick = jnp.where((jnp.broadcast_to(wanted, entry.shape) == entry) & diagonal, 1.0, 0.0)
            at = 2 * 64 * (j // 4) + 64 * n + 16 * (j % 4)
            pick_v[at : at + 16, :] = pick.astype(BF16)

    @pl.loop(1, 8)
    def _(i):
        copy1((col + i) % 8).wait_send()
        copy_s((g_me + i) % 8, g_me).wait_send()

    copy_i.wait_send()

    terms = None
    for x in range(2):
        first = (x_hi + x) % 2 * 4

        @pl.loop(first, first + 4)
        def _(g):
            @pl.when((target != g_me) | (g != g_me))
            def _():
                from2(g).wait_recv()

        grid = jnp.dot(
            recv2[pl.ds(first, 4)].reshape(4 * 32, 2 * W), table_v[...], preferred_element_type=F32
        )
        for g in range(4):
            rows = grid[32 * g : 32 * g + 32]
            re, im = (turn_v[h, pl.ds(first + g, 1), :] for h in range(2))
            term = rows[:, : 2 * S] * re + rows[:, 2 * S :] * im
            terms = term if terms is None else terms + term

    low_half = iota((16, W), 1) < 64
    for v in range(4):
        top = terms[0:16, W * v : W * v + W]
        low = terms[16:32, W * v : W * v + W]
        send3[2 * v % 4, v // 2] = jnp.where(low_half, top, pltpu.roll(low, 64, 1)).astype(BF16)
        send3[(2 * v + 1) % 4, v // 2] = jnp.where(low_half, pltpu.roll(top, 64, 1), low).astype(BF16)

    def copy3(n, dst):
        return pltpu.make_async_remote_copy(
            src_ref=send3.at[n % 4], dst_ref=recv3.at[dst], send_sem=s_3.at[n], recv_sem=r_3.at[dst],
            device_id=(facet_of(x_hi, 2 * n + zp, core), col), device_id_type=MESH,
        )

    pl.semaphore_wait(word_5, 2)
    for i in (4, 3, 5, 2, 6, 1, 7):
        copy3((zg + i) % 8, zg).start()

    total = send3[pl.ds(zg % 4, 1)].astype(F32)
    for i in (1, 7, 2, 6, 3, 5, 4):
        n = (zg + i) % 8
        copy3(n, n).wait_recv()
        total = total + recv3[pl.ds(n, 1)].astype(F32)

    place = z % 8
    recv4[pl.ds(place, 1)] = total.astype(BF16)

    def copy4(x, i, dst):
        there = 8 * x + (place + i) % 8
        return pltpu.make_async_remote_copy(
            src_ref=recv4.at[place], dst_ref=recv4.at[dst], send_sem=s_4.at[there], recv_sem=r_4.at[dst],
            device_id=(facet_of((x_hi + x) % 2, (z + i) % 16, core), col), device_id_type=MESH,
        )

    pl.semaphore_wait(word_4, 1)
    def order4(k):
        return z // 8 * (4 - k) + (1 - z // 8) * (k - 3) + 16

    for x in (1 - core, core):
        for k in range(8):

            @pl.when((x == 1) | (order4(k) != 16))
            def _():
                copy4(x, order4(k), 8 * x + place).start()


    @pl.loop(0, 8)
    def _(c):
        @pl.when((target != g_me) | (c != col))
        def _():
            copy2(c).wait_send()

    @pl.loop(1, 8)
    def _(i):
        n = (place + i) % 8
        copy4(0, i, n).wait_recv()

    half = 2 * W
    near = jnp.dot(
        pick_v[:, :half], recv4[0:8].reshape(half, W), preferred_element_type=F32
    )

    @pl.loop(0, 8)
    def _(i):
        n = (place + i) % 8
        copy4(1, i, 8 + n).wait_recv()

    def copy5(h):
        return pltpu.make_async_remote_copy(
            src_ref=send5.at[h, 1], dst_ref=recv5.at[h], send_sem=s_5.at[h], recv_sem=r_5.at[h],
            device_id=(facet_of(x_hi, z, 1 - core), col), device_id_type=MESH,
        )

    for h in range(2):
        rows = slice(W * h, W * h + W)
        picks = near[rows] + jnp.dot(
            pick_v[rows, half:], recv4[8:16].reshape(half, W), preferred_element_type=F32
        )
        send5[h] = picks.astype(BF16).reshape(2, 64, W)
        copy5(h).start()

    @pl.loop(1, 8)
    def _(i):
        copy3((zg + i) % 8, zg).wait_send()
        copy4(0, i, place).wait_send()

    @pl.loop(0, 8)
    def _(i):
        copy4(1, i, 8 + place).wait_send()

    for h in range(2):
        copy5(h).wait_recv()
        chosen = send5[h, 0].astype(F32) + recv5[h].astype(F32)
        rows = []
        for i in range(4):
            tile = chosen[16 * i : 16 * i + 16]
            other = pltpu.roll(tile, 64, 1)
            if i % 2 == 0:
                top, low = jnp.where(low_half, tile, 0.0), jnp.where(low_half, other, 0.0)
            else:
                top, low = jnp.where(low_half, 0.0, other), jnp.where(low_half, 0.0, tile)
            here = jnp.concatenate([top, low], axis=0)
            none = jnp.zeros_like(here)
            rows.append(jnp.concatenate([here, none] if i < 2 else [none, here], axis=1))
        lhs = jnp.concatenate(rows, axis=0).astype(BF16)
        deep = slice(256 * h, 256 * h + 256)
        for k in range(0, VIS, 256):
            re = jnp.dot(lhs, v_v[deep, k : k + 256], preferred_element_type=F32)
            im = jnp.dot(lhs, v_v[deep, VIS + k : VIS + k + 256], preferred_element_type=F32)
            for i in range(4):
                j = 4 * h + i
                a = (re[32 * i : 32 * i + 32], im[32 * i : 32 * i + 32])
                b = (u_v[0, j, :, k : k + 256], u_v[1, j, :, k : k + 256])
                vis = cmul(a, b)
                for part in range(2):
                    out_ref[0, 0, j, part : part + 1, k : k + 256] = jnp.sum(
                        vis[part], axis=0, keepdims=True
                    )

    copy5(0).wait_send()
    copy5(1).wait_send()


def shards(
    facet_strips, facet_offsets, column_offsets, row_offsets, tile_lists, tile_counts, uv_index
):
    anywhere = pl.BlockSpec(memory_space=pl.ANY)
    dma = pltpu.SemaphoreType.DMA
    return pl.pallas_call(
        kernel,
        out_shape=jax.ShapeDtypeStruct((1, 1, CAP, 2, VIS), F32),
        in_specs=[anywhere] * 7,
        out_specs=pl.BlockSpec(memory_space=pltpu.VMEM),
        scratch_shapes=[
            pltpu.SMEM((1, 2), I32),
            pltpu.SMEM((1,), I32),
            pltpu.SMEM((1,), I32),
            pltpu.SMEM((1, 1, CAP), I32),
            pltpu.SMEM((1, 1), I32),
            pltpu.VMEM((LEN, 2 * W), BF16),
            pltpu.VMEM((CAP, 2, VIS), I32),
            pltpu.VMEM((2 * S, LEN), BF16),
            pltpu.VMEM((8, 32, 2 * W), BF16),
            pltpu.VMEM((8, 32, 2 * W), BF16),
            pltpu.VMEM((32, 2 * W), BF16),
            pltpu.VMEM((8, 32, 2 * W), BF16),
            pltpu.VMEM((2 * W, 4 * S), BF16),
            pltpu.VMEM((4, 2, 16, W), BF16),
            pltpu.VMEM((8, 2, 16, W), BF16),
            pltpu.VMEM((16, 2, 16, W), BF16),
            pltpu.VMEM((8, W), I32),
            pltpu.VMEM((8, 8, W), I32),
            pltpu.VMEM((2, 8, 2 * S), F32),
            pltpu.VMEM((8, W), I32),
            pltpu.VMEM((8, W), I32),
            pltpu.VMEM((2 * W, 4 * W), BF16),
            pltpu.VMEM((2, 2, 64, W), BF16),
            pltpu.VMEM((2, 64, W), BF16),
            pltpu.VMEM((2, 5, 2, CAP, VIS), F32),
            pltpu.VMEM((2, CAP, TILE, VIS), F32),
            pltpu.VMEM((CAP * 64, 2 * VIS), BF16),
            dma((8,)),
            dma((8,)),
            dma((8,)),
            dma,
            dma,
            dma((8,)),
            dma((8,)),
            dma((8,)),
            dma((8,)),
            dma((8,)),
            dma((8,)),
            dma((16,)),
            dma((16,)),
            dma((2,)),
            dma((2,)),
            pltpu.SemaphoreType.REGULAR,
            pltpu.SemaphoreType.REGULAR,
            pltpu.SemaphoreType.REGULAR,
            pltpu.SemaphoreType.REGULAR,
        ],
        compiler_params=pltpu.CompilerParams(
            collective_id=0, has_side_effects=True, vmem_limit_bytes=55104 * 1024
        ),
    )(facet_strips, facet_offsets, column_offsets, row_offsets, tile_lists, tile_counts, uv_index)


def solution(mesh):
    in_specs = (
        P("facet", None, "col", None),
        P("facet", None),
        P("col"),
        P(),
        P("col", "facet", None),
        P("col", "facet"),
        P("col", "facet", None, None, None),
    )
    out_specs = P("col", "facet", None, None, None)
    return jax.shard_map(shards, mesh=mesh, in_specs=in_specs, out_specs=out_specs, check_vma=False)
```

```python
import math

import jax
import jax.numpy as jnp
from jax import lax
from jax.experimental import pallas as pl
from jax.experimental.pallas import tpu as pltpu
from jax.sharding import PartitionSpec as P

L = 8192
W = 128
S = 256
TILE = 32
NTOT = 65536
UV_STEPS = 4096
VIS = 1024
CAP = 8
FACETS = 64
LEN = 1024
MESH = pl.DeviceIdType.MESH
DEAL = 0
LINE = (4, -4, 3, -3, 2, -2)
ORDER2 = ((0, 2), (0, 1), (0, 3), (1, 2), (0, 0), (1, 1), (1, 3), (1, 0))
AROUND = (4, -3, 3, -2, 2, -1, 1, 0)
FAR = ((1, 2), (1, 1), (1, 3), (0, 2), (1, 0), (0, 1), (0, 3))
F32 = jnp.float32
BF16 = jnp.bfloat16
I32 = jnp.int32


def unit(index):
    index = index & (NTOT - 1)
    index = jnp.where(index >= NTOT // 2, index - NTOT, index)
    angle = index.astype(F32) * (2.0 * math.pi / NTOT)
    return jnp.cos(angle), jnp.sin(angle)


def cmul(a, b):
    return a[0] * b[0] - a[1] * b[1], a[0] * b[1] + a[1] * b[0]


def iota(shape, dim):
    return lax.broadcasted_iota(I32, shape, dim)


def facet_of(x_hi, z, core):
    return (x_hi * 16 + z) * 2 + core


def group_facet(g, zg):
    return facet_of(g // 4, 2 * zg + g % 2, (g // 2) % 2)


def kernel(
    strip_ref,
    offsets_hbm,
    column_hbm,
    row_hbm,
    lists_hbm,
    counts_hbm,
    uv_ref,
    out_ref,
    offsets_ref,
    column_ref,
    row_ref,
    lists_ref,
    counts_ref,
    strip_v,
    uv_v,
    left_v,
    send1,
    recv1,
    block2,
    recv2,
    table_v,
    send3,
    recv3,
    recv4,
    small_v,
    recv_s,
    turn_v,
    ids_v,
    recv_i,
    pick_v,
    send5,
    recv5,
    pow_v,
    u_v,
    v_v,
    load_sem,
    s_s,
    r_s,
    s_i,
    r_i,
    s_1,
    r_1,
    s_2,
    r_2,
    s_3,
    r_3,
    s_4,
    r_4,
    s_5,
    r_5,
    word_2,
    word_3,
    word_4,
    word_5,
):
    facet = lax.axis_index("facet")
    col = lax.axis_index("col")
    x_hi = facet // 32
    z = (facet // 2) % 16
    core = facet % 2
    zg = z // 2
    zp = z % 2
    q_me = x_hi * 2 + core
    g_me = q_me * 2 + zp
    x_lo = col // 4
    y = col % 4

    def block_of(c, x):
        return (c // 4 + x + DEAL) % 2 * 4 + c % 4

    def col_of(block, x):
        return (block // 4 + x + DEAL) % 2 * 4 + block % 4

    target = block_of(col, x_hi)

    loads = [
        pltpu.make_async_copy(strip_ref.at[0, 0], strip_v.at[:, pl.ds(0, W)], load_sem.at[0]),
        pltpu.make_async_copy(strip_ref.at[0, 1], strip_v.at[:, pl.ds(W, W)], load_sem.at[1]),
        pltpu.make_async_copy(uv_ref.at[0, 0], uv_v, load_sem.at[2]),
        pltpu.make_async_copy(offsets_hbm, offsets_ref, load_sem.at[3]),
        pltpu.make_async_copy(row_hbm, row_ref, load_sem.at[4]),
        pltpu.make_async_copy(column_hbm, column_ref, load_sem.at[5]),
        pltpu.make_async_copy(lists_hbm, lists_ref, load_sem.at[6]),
        pltpu.make_async_copy(counts_hbm, counts_ref, load_sem.at[7]),
    ]
    for n in (3, 4, 0, 1, 5, 6, 7, 2):
        loads[n].start()

    barrier = pltpu.get_barrier_semaphore()

    def greet(f, c):
        pl.semaphore_signal(barrier, inc=1, device_id=(f, c), device_id_type=MESH)

    def along(i):
        return facet_of(x_hi, (z + i + 16) % 16, core)

    def rank(p):
        return p + 4 * (p // 8 - p // 12) + p // 12 * (23 - 2 * p)

    def is_later(i):
        return (rank((z + i + 16) % 16) - rank(z) + 15) // 16

    @pl.loop(1, 8)
    def _(i):
        greet(facet, (col + i) % 8)

    @pl.loop(1, 8)
    def _(i):
        greet(group_facet((g_me + i) % 8, zg), col)

    later = 0
    for i in LINE + (2 * zp - 1,):
        later = later + is_later(i)

        @pl.when(is_later(i) == 1)
        def _():
            greet(along(i), col)

    loads[3].wait()
    loads[4].wait()

    row0 = row_ref[0]
    cells = offsets_ref[0, 0] + col * LEN + iota((8, LEN), 1)
    base = unit((row0 + 8 * iota((8, LEN), 0)) * cells)
    scale = 1.0 / math.sqrt(L)
    step = unit(64 * cells)

    def left_body(t, value):
        nxt = cmul(value, step)
        at = pl.ds(pl.multiple_of(16 * t, 16), 16)
        left_v[at, :] = jnp.concatenate([value[0], nxt[0]], axis=0).astype(BF16)
        at = pl.ds(pl.multiple_of(S + 16 * t, 16), 16)
        left_v[at, :] = jnp.concatenate([value[1], nxt[1]], axis=0).astype(BF16)
        return cmul(nxt, step)

    lax.fori_loop(0, 16, left_body, (base[0] * scale, base[1] * scale))

    loads[0].wait()
    loads[1].wait()
    both = jnp.dot(left_v[...], strip_v[...], preferred_element_type=F32)
    real = both[:S, :W] + both[S:, W:]
    imag = both[:S, W:] - both[S:, :W]
    send1[...] = jnp.concatenate([real, imag], axis=1).astype(BF16).reshape(8, 32, 2 * W)

    pl.semaphore_wait(barrier, 21 - later)

    def copy1(c):
        return pltpu.make_async_remote_copy(
            src_ref=send1.at[block_of(c, x_hi)], dst_ref=recv1.at[col], send_sem=s_1.at[c], recv_sem=r_1.at[col],
            device_id=(facet, c), device_id_type=MESH,
        )

    def from1(c):
        return pltpu.make_async_remote_copy(
            src_ref=send1.at[block_of(c, x_hi)], dst_ref=recv1.at[c], send_sem=s_1.at[c], recv_sem=r_1.at[c],
            device_id=(facet, c), device_id_type=MESH,
        )

    def col_at(far):
        return (x_lo + far[0]) % 2 * 4 + (y + far[1]) % 4

    for far in FAR:
        copy1(col_at(far)).start()

    def tell(sem, f):
        pl.semaphore_signal(sem, inc=1, device_id=(f, col), device_id_type=MESH)

    for g in range(8):

        @pl.when((block_of(col, g // 4) == g_me) & (g != g_me))
        def _():
            tell(word_2, group_facet(g, zg))

    for i in LINE + (2 * zp - 1,):

        @pl.when(is_later(i) == 0)
        def _():
            tell(word_3, along(i))

    loads[6].wait()
    loads[7].wait()
    lanes = iota((8, W), 0)
    ids = jnp.full((8, W), -1, I32)
    for j in range(CAP):
        ids = jnp.where((lanes == j) & (j < counts_ref[0, 0]), lists_ref[0, 0, j], ids)
    ids_v[...] = ids
    small_v[...] = jnp.full((8, W), offsets_ref[0, 1], I32)
    recv_s[pl.ds(g_me, 1)] = small_v[...][None]

    def copy_s(g, dst):
        return pltpu.make_async_remote_copy(
            src_ref=small_v, dst_ref=recv_s.at[dst], send_sem=s_s.at[g], recv_sem=r_s.at[dst],
            device_id=(group_facet(g, zg), col), device_id_type=MESH,
        )

    copy_i = pltpu.make_async_remote_copy(
        src_ref=ids_v, dst_ref=recv_i, send_sem=s_i, recv_sem=r_i,
        device_id=(facet_of(x_hi, z, 1 - core), col), device_id_type=MESH,
    )
    copy_i.start()

    @pl.loop(1, 8)
    def _(i):
        copy_s((g_me + i) % 8, g_me).start()

    loads[5].wait()
    lane = iota((8, 2 * S), 1)
    sample = column_ref[0] + 256 * (32 * (lane // 64) + lane % 32)
    quarter = (NTOT // 4) * ((lane // 32) % 2)
    base_r = unit(iota((8, 2 * S), 0) * sample + quarter)
    step_r = unit(8 * sample)

    def right_body(t, value):
        nxt = cmul(value, step_r)
        re = jnp.concatenate([value[0], nxt[0]], axis=0)
        im = jnp.concatenate([value[1], nxt[1]], axis=0)
        top = pl.ds(pl.multiple_of(16 * t, 16), 16)
        low = pl.ds(pl.multiple_of(W + 16 * t, 16), 16)
        table_v[top, 0 : 2 * S] = re.astype(BF16)
        table_v[low, 0 : 2 * S] = im.astype(BF16)
        table_v[top, 2 * S :] = (-im).astype(BF16)
        table_v[low, 2 * S :] = re.astype(BF16)
        return cmul(nxt, step_r)

    lax.fori_loop(0, 8, right_body, base_r)

    total = send1[pl.ds(target, 1)].astype(F32)
    for far in FAR[::-1]:
        c = col_at(far)
        from1(c).wait_recv()
        total = total + recv1[pl.ds(c, 1)].astype(F32)
    block2[...] = total[0].astype(BF16)

    def copy2(c):
        return pltpu.make_async_remote_copy(
            src_ref=block2, dst_ref=recv2.at[g_me], send_sem=s_2.at[c], recv_sem=r_2.at[g_me],
            device_id=(group_facet(target, zg), c), device_id_type=MESH,
        )

    def from2(g):
        return pltpu.make_async_remote_copy(
            src_ref=block2, dst_ref=recv2.at[g], send_sem=s_2.at[g], recv_sem=r_2.at[g],
            device_id=(group_facet(g, zg), col_of(g_me, g // 4)), device_id_type=MESH,
        )

    @pl.when(target != g_me)
    def _():
        pl.semaphore_wait(word_2, 1)

    for x, dy in ORDER2:
        c = 4 * x + (y + dy) % 4

        @pl.when((target != g_me) | (c != col))
        def _():
            copy2(c).start()

    @pl.when(target == g_me)
    def _():
        recv2[pl.ds(g_me, 1)] = block2[...][None]

    @pl.when(later > 0)
    def _():
        pl.semaphore_wait(word_3, later)

    tell(word_5, along(4))
    tell(word_5, along(-4))
    tell(word_4, facet_of(1 - x_hi, z, core))

    loads[2].wait()
    for part in range(2):
        index = jnp.concatenate([uv_v[j, part : part + 1, :] for j in range(CAP)], axis=0)
        value = unit(index * (NTOT // UV_STEPS))
        for k in range(5):
            pow_v[part, k, 0] = value[0]
            pow_v[part, k, 1] = value[1]
            value = cmul(value, value)

    sub = iota((8, VIS), 0)

    def powers(part, j):
        def power(k):
            return tuple(
                jnp.broadcast_to(pow_v[part, k, h, pl.ds(j, 1), :], (8, VIS)) for h in range(2)
            )

        def chosen_power(k):
            re, im = power(k)
            on = (sub & (1 << k)) != 0
            return jnp.where(on, re, 1.0), jnp.where(on, im, 0.0)

        low = cmul(cmul(chosen_power(0), chosen_power(1)), chosen_power(2))
        sixteen = power(4)
        second = cmul(low, power(3))
        third = cmul(low, sixteen)
        fourth = cmul(second, sixteen)
        parts = (low, second, third, fourth)
        return tuple(jnp.concatenate([p[h] for p in parts], axis=0) for h in range(2))

    @pl.loop(0, CAP)
    def _(j):
        re, im = powers(0, j)
        u_v[0, j] = re * (1.0 / TILE)
        u_v[1, j] = im * (1.0 / TILE)
        re, im = powers(1, j)
        top = pl.ds(pl.multiple_of(64 * j, 32), 32)
        low = pl.ds(pl.multiple_of(64 * j + 32, 32), 32)
        v_v[top, 0:VIS] = re.astype(BF16)
        v_v[top, VIS:] = im.astype(BF16)
        v_v[low, 0:VIS] = (-im).astype(BF16)
        v_v[low, VIS:] = re.astype(BF16)

    @pl.loop(1, 8)
    def _(i):
        copy_s((g_me + i) % 8, (g_me + i) % 8).wait_recv()

    across = jnp.zeros((8, W), I32)
    for g in range(8):
        across = jnp.where(lanes == g, recv_s[g], across)
    across = jnp.concatenate([across] * 4, axis=1)
    turn = unit(across * sample)
    norm = 1.0 / math.sqrt(W * FACETS)
    turn_v[0] = turn[0] * norm
    turn_v[1] = turn[1] * norm

    copy_i.wait_recv()
    entry = iota((16, 4 * W), 1)
    diagonal = iota((16, 4 * W), 0) == entry % 16
    entry = entry // 16
    at_place = entry // 2 % 8
    entry = 32 * ((entry // 16 + x_hi) % 2) + 16 * core + 8 * (at_place % 2) + at_place // 2 + 4 * (entry % 2)
    for n, wanted_ref in enumerate((ids_v, recv_i)):
        for j in range(CAP):
            wanted = jnp.concatenate([wanted_ref[j : j + 1, :]] * 4, axis=1)
            pick = jnp.where((jnp.broadcast_to(wanted, entry.shape) == entry) & diagonal, 1.0, 0.0)
            at = 2 * 64 * (j // 4) + 64 * n + 16 * (j % 4)
            pick_v[at : at + 16, :] = pick.astype(BF16)

    @pl.loop(1, 8)
    def _(i):
        copy1((col + i) % 8).wait_send()
        copy_s((g_me + i) % 8, g_me).wait_send()

    copy_i.wait_send()

    terms = None
    for x, skip, many in ((0, 0, 4), (1, 0, 2), (1, 2, 2)):
        first = (x_hi + x) % 2 * 4 + skip

        @pl.loop(first, first + many)
        def _(g):
            @pl.when((target != g_me) | (g != g_me))
            def _():
                from2(g).wait_recv()

        grid = jnp.dot(
            recv2[pl.ds(first, many)].reshape(many * 32, 2 * W), table_v[...], preferred_element_type=F32
        )
        for g in range(many):
            rows = grid[32 * g : 32 * g + 32]
            re, im = (turn_v[h, pl.ds(first + g, 1), :] for h in range(2))
            term = rows[:, : 2 * S] * re + rows[:, 2 * S :] * im
            terms = term if terms is None else terms + term

    low_half = iota((16, W), 1) < 64
    for v in range(4):
        top = terms[0:16, W * v : W * v + W]
        low = terms[16:32, W * v : W * v + W]
        send3[2 * v % 4, v // 2] = jnp.where(low_half, top, pltpu.roll(low, 64, 1)).astype(BF16)
        send3[(2 * v + 1) % 4, v // 2] = jnp.where(low_half, pltpu.roll(top, 64, 1), low).astype(BF16)

    def copy3(n, dst):
        return pltpu.make_async_remote_copy(
            src_ref=send3.at[n % 4], dst_ref=recv3.at[dst], send_sem=s_3.at[n], recv_sem=r_3.at[dst],
            device_id=(facet_of(x_hi, 2 * n + zp, core), col), device_id_type=MESH,
        )

    pl.semaphore_wait(word_5, 2)
    for i in (4, 3, 5, 2, 6, 1, 7):
        copy3((zg + i) % 8, zg).start()

    total = send3[pl.ds(zg % 4, 1)].astype(F32)
    for i in (1, 7, 2, 6, 3, 5, 4):
        n = (zg + i) % 8
        copy3(n, n).wait_recv()
        total = total + recv3[pl.ds(n, 1)].astype(F32)

    place = z % 8
    recv4[pl.ds(place, 1)] = total.astype(BF16)

    def copy4(x, i, dst):
        there = 8 * x + (place + i) % 8
        return pltpu.make_async_remote_copy(
            src_ref=recv4.at[place], dst_ref=recv4.at[dst], send_sem=s_4.at[there], recv_sem=r_4.at[dst],
            device_id=(facet_of((x_hi + x) % 2, (z + i) % 16, core), col), device_id_type=MESH,
        )

    pl.semaphore_wait(word_4, 1)
    for i in AROUND:
        copy4(1, i + 16, 8 + place).start()
    for i in AROUND[:-1]:
        copy4(0, i + 16, place).start()

    @pl.loop(0, 8)
    def _(c):
        @pl.when((target != g_me) | (c != col))
        def _():
            copy2(c).wait_send()

    @pl.loop(1, 8)
    def _(i):
        n = (place + i) % 8
        copy4(0, i, n).wait_recv()

    half = 2 * W
    near = jnp.dot(
        pick_v[:, :half], recv4[0:8].reshape(half, W), preferred_element_type=F32
    )

    @pl.loop(0, 8)
    def _(i):
        n = (place + i) % 8
        copy4(1, i, 8 + n).wait_recv()

    def copy5(h):
        return pltpu.make_async_remote_copy(
            src_ref=send5.at[h, 1], dst_ref=recv5.at[h], send_sem=s_5.at[h], recv_sem=r_5.at[h],
            device_id=(facet_of(x_hi, z, 1 - core), col), device_id_type=MESH,
        )

    for h in range(2):
        rows = slice(W * h, W * h + W)
        picks = near[rows] + jnp.dot(
            pick_v[rows, half:], recv4[8:16].reshape(half, W), preferred_element_type=F32
        )
        send5[h] = picks.astype(BF16).reshape(2, 64, W)
        copy5(h).start()

    @pl.loop(1, 8)
    def _(i):
        copy3((zg + i) % 8, zg).wait_send()
        copy4(0, i, place).wait_send()

    @pl.loop(0, 8)
    def _(i):
        copy4(1, i, 8 + place).wait_send()

    for h in range(2):
        copy5(h).wait_recv()
        chosen = send5[h, 0].astype(F32) + recv5[h].astype(F32)
        rows = []
        for i in range(4):
            tile = chosen[16 * i : 16 * i + 16]
            other = pltpu.roll(tile, 64, 1)
            if i % 2 == 0:
                top, low = jnp.where(low_half, tile, 0.0), jnp.where(low_half, other, 0.0)
            else:
                top, low = jnp.where(low_half, 0.0, other), jnp.where(low_half, 0.0, tile)
            here = jnp.concatenate([top, low], axis=0)
            none = jnp.zeros_like(here)
            rows.append(jnp.concatenate([here, none] if i < 2 else [none, here], axis=1))
        lhs = jnp.concatenate(rows, axis=0).astype(BF16)
        deep = slice(256 * h, 256 * h + 256)
        for k in range(0, VIS, 256):
            re = jnp.dot(lhs, v_v[deep, k : k + 256], preferred_element_type=F32)
            im = jnp.dot(lhs, v_v[deep, VIS + k : VIS + k + 256], preferred_element_type=F32)
            for i in range(4):
                j = 4 * h + i
                a = (re[32 * i : 32 * i + 32], im[32 * i : 32 * i + 32])
                b = (u_v[0, j, :, k : k + 256], u_v[1, j, :, k : k + 256])
                vis = cmul(a, b)
                for part in range(2):
                    out_ref[0, 0, j, part : part + 1, k : k + 256] = jnp.sum(
                        vis[part], axis=0, keepdims=True
                    )

    copy5(0).wait_send()
    copy5(1).wait_send()


def shards(
    facet_strips, facet_offsets, column_offsets, row_offsets, tile_lists, tile_counts, uv_index
):
    anywhere = pl.BlockSpec(memory_space=pl.ANY)
    dma = pltpu.SemaphoreType.DMA
    return pl.pallas_call(
        kernel,
        out_shape=jax.ShapeDtypeStruct((1, 1, CAP, 2, VIS), F32),
        in_specs=[anywhere] * 7,
        out_specs=pl.BlockSpec(memory_space=pltpu.VMEM),
        scratch_shapes=[
            pltpu.SMEM((1, 2), I32),
            pltpu.SMEM((1,), I32),
            pltpu.SMEM((1,), I32),
            pltpu.SMEM((1, 1, CAP), I32),
            pltpu.SMEM((1, 1), I32),
            pltpu.VMEM((LEN, 2 * W), BF16),
            pltpu.VMEM((CAP, 2, VIS), I32),
            pltpu.VMEM((2 * S, LEN), BF16),
            pltpu.VMEM((8, 32, 2 * W), BF16),
            pltpu.VMEM((8, 32, 2 * W), BF16),
            pltpu.VMEM((32, 2 * W), BF16),
            pltpu.VMEM((8, 32, 2 * W), BF16),
            pltpu.VMEM((2 * W, 4 * S), BF16),
            pltpu.VMEM((4, 2, 16, W), BF16),
            pltpu.VMEM((8, 2, 16, W), BF16),
            pltpu.VMEM((16, 2, 16, W), BF16),
            pltpu.VMEM((8, W), I32),
            pltpu.VMEM((8, 8, W), I32),
            pltpu.VMEM((2, 8, 2 * S), F32),
            pltpu.VMEM((8, W), I32),
            pltpu.VMEM((8, W), I32),
            pltpu.VMEM((2 * W, 4 * W), BF16),
            pltpu.VMEM((2, 2, 64, W), BF16),
            pltpu.VMEM((2, 64, W), BF16),
            pltpu.VMEM((2, 5, 2, CAP, VIS), F32),
            pltpu.VMEM((2, CAP, TILE, VIS), F32),
            pltpu.VMEM((CAP * 64, 2 * VIS), BF16),
            dma((8,)),
            dma((8,)),
            dma((8,)),
            dma,
            dma,
            dma((8,)),
            dma((8,)),
            dma((8,)),
            dma((8,)),
            dma((8,)),
            dma((8,)),
            dma((16,)),
            dma((16,)),
            dma((2,)),
            dma((2,)),
            pltpu.SemaphoreType.REGULAR,
            pltpu.SemaphoreType.REGULAR,
            pltpu.SemaphoreType.REGULAR,
            pltpu.SemaphoreType.REGULAR,
        ],
        compiler_params=pltpu.CompilerParams(
            collective_id=0, has_side_effects=True, vmem_limit_bytes=55104 * 1024
        ),
    )(facet_strips, facet_offsets, column_offsets, row_offsets, tile_lists, tile_counts, uv_index)


def solution(mesh):
    in_specs = (
        P("facet", None, "col", None),
        P("facet", None),
        P("col"),
        P(),
        P("col", "facet", None),
        P("col", "facet"),
        P("col", "facet", None, None, None),
    )
    out_specs = P("col", "facet", None, None, None)
    return jax.shard_map(shards, mesh=mesh, in_specs=in_specs, out_specs=out_specs, check_vma=False)
```
